32 devices in a mesh: gy: 8 (over y, x, core), gz: 4 (over z).
Axes of the slice: x: 2, y: 2, z: 4, core: 2. Of those that a mesh axis runs over, the one named last changes fastest.
Arguments:
- coarse: float32 [8, 1, 256, 256], P(None, None, 'gy', 'gz'), may hold values from 0 to 1
- labels: int32 [2, 512, 512], P(None, 'gy', 'gz'), may hold values from 0 to 7
- mobility: float32 [8], replicated, may hold values from 0.5 to 2
Outputs:
- phase_field: float32 [8, 2, 512, 512], P(None, None, 'gy', 'gz')
The draws below stay inside these ranges and needn't reach their ends.
All inputs are finite; a program needn't handle non-finite values.
Results may differ from the reference program's by a relative error of at most 0.0001.
Values sent between devices are 32-bit elements; how exact they have to be, the bound alone decides.
A program may use at most 64 MiB of HBM per device.

```python
import math
import jax
import jax.numpy as jnp
from jax import lax

P_SIZE = 8
CX = 1
ITERS = 2
FX = 2
CNY = 256
CNZ = 256
NY = 512
NZ = 512


def with_ends(entries, rng, low, largest):
    longest = entries.shape.index(max(entries.shape))
    spots = []
    for shift in (0, 1):
        where = [jax.random.randint(jax.random.fold_in(rng, axis), (), 0, length) for axis, length in enumerate(entries.shape)]
        where[longest] = (where[longest] + shift) % entries.shape[longest]
        spots.append(tuple(where))
    return entries.at[spots[0]].set(low).at[spots[1]].set(largest)


def block_scale(stream_key, dims, shards, least, largest):
    def one(position, parts):
        draws = jax.random.uniform(jax.random.fold_in(jax.random.fold_in(stream_key, 6), position), (parts,), jnp.float32, least / len(shards), largest / len(shards))
        return jnp.repeat(jnp.exp(draws), dims[position] // parts).reshape((-1,) + (1,) * (len(dims) - position - 1))

    gain = one(*shards[0])
    for cut in shards[1:]:
        gain = gain * one(*cut)
    return gain


def setup_inputs(seed: int = 0) -> dict:
    key_of = jax.random.split(jax.random.key(seed), 4)
    return {
        "coarse": jnp.clip(1.0 * jax.random.uniform(key_of[0], (P_SIZE, CX, CNY, CNZ), jnp.float32) ** block_scale(key_of[0], (P_SIZE, CX, CNY, CNZ), ((2, 8), (3, 4)), -0.2, 0.2), 0.0, 1.0),
        "labels": with_ends(jax.random.randint(key_of[1], (FX, NY, NZ), 0, P_SIZE), jax.random.fold_in(key_of[1], 1), 0, P_SIZE - 1).astype(jnp.int32),
        "mobility": jnp.clip(jnp.exp(jax.random.uniform(key_of[2], (P_SIZE,), jnp.float32, math.log(0.5), math.log(2.0))), 0.5, 2.0),
    }


STEP = 0.075
GAMMA = 0.5
PIN = 1.0


def refine(field, axis):
    count = field.shape[axis]
    lower = lax.slice_in_dim(field, 0, count - 1, axis=axis)
    upper = lax.slice_in_dim(field, 1, count, axis=axis)
    odd_cells = 0.75 * lower + 0.25 * upper
    even_cells = 0.75 * upper + 0.25 * lower
    paired = jnp.stack([odd_cells, even_cells], axis=axis + 1)
    shape = list(field.shape)
    shape[axis] = 2 * (count - 1)
    return paired.reshape(shape)


def advance(padded, labels, mobility):
    center = padded[:, :, 1:-1, 1:-1]
    lap = jnp.roll(center, 1, 1) + jnp.roll(center, -1, 1)
    lap = lap + padded[:, :, 2:, 1:-1] + padded[:, :, :-2, 1:-1]
    lap = lap + padded[:, :, 1:-1, 2:] + padded[:, :, 1:-1, :-2] - 6.0 * center
    phases = jnp.arange(center.shape[0], dtype=jnp.int32)
    onehot = (labels[None] == phases[:, None, None, None]).astype(jnp.float32)
    squared = center * center
    squares = jnp.sum(squared, axis=0, keepdims=True)
    drive = center * (1.0 - squared) - 2.0 * GAMMA * center * (squares - squared) + PIN * (onehot - center)
    return center + STEP * mobility[:, None, None, None] * (lap + drive)


def reference(coarse, labels, mobility):
    padded = jnp.pad(coarse, ((0, 0), (1, 1), (1, 1), (1, 1)), mode="wrap")
    fine = refine(refine(refine(padded, 1), 2), 3)
    phase = fine[:, 1:-1, 1:-1, 1:-1]
    for step in range(ITERS):
        wrapped = jnp.pad(phase, ((0, 0), (0, 0), (1, 1), (1, 1)), mode="wrap")
        phase = advance(wrapped, labels, mobility)
    return phase
```

```python
import functools

import jax
import jax.numpy as jnp
import numpy as np
from jax import lax
from jax.experimental import pallas as pl
from jax.experimental.pallas import tpu as pltpu
from jax.sharding import PartitionSpec as P

STEP = 0.075
MESH = pl.DeviceIdType.MESH
F32 = jnp.float32
BF16 = jnp.bfloat16


def taps(cell):
    i = cell // 2
    return ((i, 0.75), (i + 1 if cell % 2 else i - 1, 0.25))


def col_lane(col, nz):
    return col % (2 * nz)


def main_operator(nz):
    width = 2 * nz
    w = np.zeros((width, width), np.float32)
    for z in range(width):
        for c, a in taps(z):
            w[col_lane(c, nz), z] += a
    return w


def strip_operator(ny, nz):
    width = 2 * nz

    def where(r, c):
        if r == -1:
            return 2 * width + col_lane(c, nz)
        if r == ny:
            return 2 * width + (col_lane(c, nz) + 8) % width
        assert 0 <= r < ny
        if c in (0, 1):
            return 2 * r + c
        if c in (nz - 2, nz - 1):
            return 2 * ny + 2 * r + c - (nz - 2)
        if c in (nz, nz + 1):
            return width + 2 * r + c - nz
        assert c in (-2, -1)
        return width + 2 * ny + 2 * r + c + 2

    w = np.zeros((3 * width, 4 * width), np.float32)

    def put(y, z, out):
        for r, a in taps(y):
            for c, b in taps(z):
                w[where(r, c), out] += a * b

    for y in range(2 * ny):
        left, right = 2 * y, (2 * y - 1) % width
        for block, (zl, zr) in enumerate(((-2, width + 1), (-1, width), (0, width - 1))):
            put(y, zl, block * width + left)
            put(y, zr, block * width + right)
    put(-1, -1, 3 * width)
    put(-1, width, 3 * width + width - 1)
    put(2 * ny, -1, 3 * width + width - 2)
    put(2 * ny, width, 3 * width + width - 3)
    return w


def label_operator(ny, nz):
    width = 2 * nz
    w = np.zeros((2 * width, 2 * width), np.float32)
    for x in range(2):
        for y in range(2 * ny):
            w[x * 2 * ny + y, x * width + 2 * y] = 1
            w[width + x * 2 * ny + y, x * width + (2 * y - 1) % width] = 1
    return w


PARTS = (
    ((-1, 0), (0, 3), (0, 3)),
    ((1, 0), (3, 6), (3, 6)),
    ((0, -1), (6, 8), (6, 8)),
    ((0, 1), (8, 10), (8, 10)),
    ((-1, -1), (0, 2), (10, 12)),
    ((-1, 1), (0, 2), (12, 14)),
    ((1, -1), (3, 5), (14, 16)),
    ((1, 1), (3, 5), (16, 18)),
)
SLOTS = 19


def wide(x):
    return jnp.concatenate([x, jnp.zeros_like(x)], axis=-1)


def exchange(gy, gz, coarse_ref, labels_ref, out_ref, stage, send_sem, recv_sem):
    me_y, me_z = lax.axis_index("gy"), lax.axis_index("gz")

    def other(dy, dz):
        return (lax.rem(me_y + dy + gy, gy), lax.rem(me_z + dz + gz, gz))

    barrier = pltpu.get_barrier_semaphore()
    for (dy, dz), _, _ in PARTS:
        pl.semaphore_signal(barrier, inc=1, device_id=other(dy, dz), device_id_type=MESH)

    phases, _, ny, nz = coarse_ref.shape
    width = 2 * nz
    x = jnp.swapaxes(coarse_ref[:, 0], 0, 1)
    rows = [wide(x[r]) for r in range(ny)]
    lane = lax.broadcasted_iota(jnp.int32, (phases, width), 1)
    left = jnp.zeros((phases, width), F32)
    right = jnp.zeros((phases, width), F32)
    for r in range(ny):
        turned = rows[r] if r == 0 else pltpu.roll(rows[r], 2 * r, 1)
        left = jnp.where((lane >= 2 * r) & (lane < 2 * r + 2), turned, left)
        low = nz - 2 + 2 * r
        right = jnp.where((lane >= low) & (lane < low + 2), turned, right)
    right = pltpu.roll(right, (2 * ny - (nz - 2)) % width, 1)

    labels = labels_ref[...].astype(F32)
    flat = labels.reshape(-1, width)
    pick_lane = lax.broadcasted_iota(jnp.int32, (phases, width), 1)

    def column(z):
        pick = (pick_lane == z).astype(BF16)
        return lax.dot_general(
            pick, flat.astype(BF16), (((1,), (1,)), ((), ())), preferred_element_type=F32
        )

    stage[0] = rows[0]
    stage[1] = rows[1]
    stage[2, 0:2] = labels[:, 0]
    stage[3] = rows[ny - 2]
    stage[4] = rows[ny - 1]
    stage[5, 0:2] = labels[:, 2 * ny - 1]
    stage[6] = left
    stage[7] = column(0)
    stage[8] = right
    stage[9] = column(width - 1)
    out_ref[SLOTS - 1] = left + right

    pl.semaphore_wait(barrier, len(PARTS))
    copies = []
    for n, ((dy, dz), (s0, s1), (d0, d1)) in enumerate(PARTS):
        copy = pltpu.make_async_remote_copy(
            src_ref=stage.at[s0:s1],
            dst_ref=out_ref.at[d0:d1],
            send_sem=send_sem.at[n],
            recv_sem=recv_sem.at[n],
            device_id=other(dy, dz),
            device_id_type=MESH,
        )
        copy.start()
        copies.append(copy)
    for copy in copies:
        copy.wait()


def exact_dot(x, w):
    high = x.astype(BF16)
    low = (x - high.astype(F32)).astype(BF16)
    return jnp.dot(high, w, preferred_element_type=F32) + jnp.dot(low, w, preferred_element_type=F32)


def relax(coarse_ref, labels_ref, mobility_ref, got, main_ref, strip_ref, label_ref, out_ref, p1):
    phases, _, ny, nz = coarse_ref.shape
    width = 2 * nz
    fy = 2 * ny
    shape = (phases, width)
    lane = lax.broadcasted_iota(jnp.int32, shape, 1)
    phase_id = lax.broadcasted_iota(jnp.int32, shape, 0)
    phase_f = phase_id.astype(F32)
    rate = jnp.zeros(shape, F32)
    for p in range(phases):
        rate = jnp.where(phase_id == p, STEP * mobility_ref[p], rate)
    first, last = lane == 0, lane == width - 1
    ends = first | last

    def turn(v, by):
        return pltpu.roll(v, by % width, 1) if by % width else v

    def total(v):
        return jnp.broadcast_to(jnp.sum(v * v, axis=0, keepdims=True), shape)

    def around(c, side):
        return jnp.where(first, side, turn(c, 1)) + jnp.where(last, side, turn(c, -1))

    halo_right = (lane >= nz) & (lane < nz + 2)
    halo_left = lane >= width - 2

    def edge(row, from_left, from_right, left_by=nz, right_by=nz):
        v = jnp.where(halo_right, turn(from_right, right_by), row)
        return jnp.where(halo_left, turn(from_left, left_by), v)

    below = [edge(got[n], got[12 + n], got[10 + n]) for n in range(2)]
    above = [edge(got[3 + n], got[16 + n], got[14 + n]) for n in range(2)]
    x = jnp.swapaxes(coarse_ref[:, 0], 0, 1)
    x = jnp.concatenate([x, jnp.zeros_like(x)], axis=-1)
    top = edge(x[0], got[8], got[6], width - 2 - 2 * ny, nz)
    low = 2 * (ny - 1)
    bottom = edge(x[ny - 1], got[8], got[6], width - 2 - 2 * ny - low, nz - low)
    rows = jnp.concatenate(
        [jnp.stack([*above, top]), x[1 : ny - 1], jnp.stack([bottom, *below])], axis=0
    )
    fine_z = exact_dot(rows.reshape(-1, width), main_ref[...]).reshape(ny + 4, phases, width)

    beside = jnp.where(lane < 2 * ny, got[6], got[8])
    near = (lane < 4) | (lane >= nz - 4) & (lane < nz + 4) | (lane >= width - 4)
    rim = jnp.where(near, above[1], turn(below[0], 8))
    strips = exact_dot(jnp.concatenate([got[SLOTS - 1], beside, rim], axis=1), strip_ref[...])
    outer, side, inner, corner = (strips[:, n * width : (n + 1) * width] for n in range(4))
    near_labels = jnp.concatenate([got[9], got[7]], axis=1).astype(BF16)
    strip_labels = jnp.dot(near_labels, label_ref[...], preferred_element_type=F32)
    up = jnp.where(ends, corner, turn(side, 2))
    down = jnp.where((lane == width - 2) | (lane == width - 3), corner, turn(side, -2))
    side_base = side + rate * (outer + inner + up + down - side * (4.0 + total(side)))
    side1 = [
        side_base + jnp.where(strip_labels[:, n * width : (n + 1) * width] == phase_f, rate, 0.0)
        for n in range(2)
    ]

    def fine_row(y):
        (r0, a), (r1, b) = taps(y)
        v = a * fine_z[r0 + 2] + b * fine_z[r1 + 2]
        return jnp.where(ends, turn(inner, -2 * y), v) if 0 <= y < fy else v

    def label_row(n, y):
        if y < 0:
            row = got[5, n : n + 1]
        elif y >= fy:
            row = got[2, n : n + 1]
        else:
            return jnp.broadcast_to(labels_ref[n, y : y + 1], shape) == phase_id
        return jnp.broadcast_to(row, shape) == phase_f

    def pinned(n, y):
        return jnp.where(label_row(n, y), rate, 0.0)

    prev, cur = fine_row(-2), fine_row(-1)
    for y in range(-1, fy + 1):
        nxt = fine_row(y + 1)
        if y < 0:
            beside_row = corner
        elif y == fy:
            beside_row = turn(corner, 2)
        else:
            beside_row = turn(side, -2 * y)
        base = cur + rate * (prev + nxt + around(cur, beside_row) - cur * (4.0 + total(cur)))
        for n in range(2):
            p1[n, y + 1] = base + pinned(n, y)
        prev, cur = cur, nxt

    for block in range(fy // 8):
        done = [[], []]
        for y in range(8 * block, 8 * block + 8):
            both = [p1[n, y + 1] for n in range(2)]
            for n in range(2):
                c = both[n]
                near = p1[n, y] + p1[n, y + 2] + around(c, turn(side1[n], -2 * y))
                near = near + 2.0 * both[1 - n]
                done[n].append(c + rate * (near - c * (6.0 + total(c))) + pinned(n, y))
        for n in range(2):
            out_ref[:, n, 8 * block : 8 * block + 8] = jnp.swapaxes(jnp.stack(done[n]), 0, 1)


def shards(gy, gz, coarse, labels, mobility):
    phases, planes, ny, nz = coarse.shape
    assert planes == 1 and labels.shape == (2, 2 * ny, 2 * nz) and ny <= nz // 2 and phases == 8
    width = 2 * nz
    vmem = pl.BlockSpec(memory_space=pltpu.VMEM)
    got = pl.pallas_call(
        functools.partial(exchange, gy, gz),
        out_shape=jax.ShapeDtypeStruct((SLOTS, phases, width), F32),
        in_specs=[vmem] * 2,
        out_specs=vmem,
        scratch_shapes=[
            pltpu.VMEM((10, phases, width), F32),
            pltpu.SemaphoreType.DMA((len(PARTS),)),
            pltpu.SemaphoreType.DMA((len(PARTS),)),
        ],
        compiler_params=pltpu.CompilerParams(collective_id=0, has_side_effects=True),
        name="exchange",
    )(coarse, labels)
    weights = [
        jnp.asarray(w, BF16)
        for w in (main_operator(nz), strip_operator(ny, nz), label_operator(ny, nz))
    ]
    return pl.pallas_call(
        relax,
        out_shape=jax.ShapeDtypeStruct((phases, 2, 2 * ny, width), F32),
        in_specs=[vmem] * 2 + [pl.BlockSpec(memory_space=pltpu.SMEM)] + [vmem] * 4,
        out_specs=vmem,
        scratch_shapes=[pltpu.VMEM((2, 2 * ny + 2, phases, width), F32)],
        compiler_params=pltpu.CompilerParams(vmem_limit_bytes=16 * 2**20),
        name="relax",
    )(coarse, labels, mobility, got, *weights)


def solution(mesh):
    in_specs = (P(None, None, "gy", "gz"), P(None, "gy", "gz"), P())
    out_specs = P(None, None, "gy", "gz")
    fn = functools.partial(shards, mesh.shape["gy"], mesh.shape["gz"])
    return jax.shard_map(fn, mesh=mesh, in_specs=in_specs, out_specs=out_specs, check_vma=False)
```

```python
import functools

import jax
import jax.numpy as jnp
import numpy as np
from jax import lax
from jax.experimental import pallas as pl
from jax.experimental.pallas import tpu as pltpu
from jax.sharding import PartitionSpec as P

STEP = 0.075
MESH = pl.DeviceIdType.MESH
F32 = jnp.float32
BF16 = jnp.bfloat16


def taps(cell):
    i = cell // 2
    return ((i, 0.75), (i + 1 if cell % 2 else i - 1, 0.25))


def col_lane(col, nz):
    return col % (2 * nz)


def main_operator(nz):
    width = 2 * nz
    w = np.zeros((width, width), np.float32)
    for z in range(width):
        for c, a in taps(z):
            w[col_lane(c, nz), z] += a
    return w


def strip_operator(ny, nz):
    width = 2 * nz

    def where(r, c):
        if r == -1:
            return 2 * width + col_lane(c, nz)
        if r == ny:
            return 2 * width + (col_lane(c, nz) + 8) % width
        assert 0 <= r < ny
        if c in (0, 1):
            return 2 * r + c
        if c in (nz - 2, nz - 1):
            return 2 * ny + 2 * r + c - (nz - 2)
        if c in (nz, nz + 1):
            return width + 2 * r + c - nz
        assert c in (-2, -1)
        return width + 2 * ny + 2 * r + c + 2

    w = np.zeros((3 * width, 4 * width), np.float32)

    def put(y, z, out):
        for r, a in taps(y):
            for c, b in taps(z):
                w[where(r, c), out] += a * b

    for y in range(2 * ny):
        left, right = 2 * y, (2 * y - 1) % width
        for block, (zl, zr) in enumerate(((-2, width + 1), (-1, width), (0, width - 1))):
            put(y, zl, block * width + left)
            put(y, zr, block * width + right)
    put(-1, -1, 3 * width)
    put(-1, width, 3 * width + width - 1)
    put(2 * ny, -1, 3 * width + width - 2)
    put(2 * ny, width, 3 * width + width - 3)
    return w


def label_operator(ny, nz):
    width = 2 * nz
    w = np.zeros((2 * width, 2 * width), np.float32)
    for x in range(2):
        for y in range(2 * ny):
            w[x * 2 * ny + y, x * width + 2 * y] = 1
            w[width + x * 2 * ny + y, x * width + (2 * y - 1) % width] = 1
    return w


PARTS = (
    ((-1, 0), (0, 3), (0, 3)),
    ((1, 0), (3, 6), (3, 6)),
    ((0, -1), (6, 8), (6, 8)),
    ((0, 1), (8, 10), (8, 10)),
    ((-1, -1), (0, 2), (10, 12)),
    ((-1, 1), (0, 2), (12, 14)),
    ((1, -1), (3, 5), (14, 16)),
    ((1, 1), (3, 5), (16, 18)),
)
SLOTS = 19


def wide(x):
    return jnp.concatenate([x, jnp.zeros_like(x)], axis=-1)


def exchange(
    gy, gz, coarse_hbm, labels_hbm, out_ref, coarse_ref, labels_ref, stage, send_sem, recv_sem, load_sem
):
    me_y, me_z = lax.axis_index("gy"), lax.axis_index("gz")

    def other(dy, dz):
        return (lax.rem(me_y + dy + gy, gy), lax.rem(me_z + dz + gz, gz))

    barrier = pltpu.get_barrier_semaphore()
    for (dy, dz), _, _ in PARTS:
        pl.semaphore_signal(barrier, inc=1, device_id=other(dy, dz), device_id_type=MESH)
    loads = [
        pltpu.make_async_copy(coarse_hbm, coarse_ref, load_sem.at[0]),
        pltpu.make_async_copy(labels_hbm, labels_ref, load_sem.at[1]),
    ]
    for load in loads:
        load.start()
    for load in loads:
        load.wait()

    phases, _, ny, nz = coarse_ref.shape
    width = 2 * nz
    x = jnp.swapaxes(coarse_ref[:, 0], 0, 1)
    rows = [wide(x[r]) for r in range(ny)]
    lane = lax.broadcasted_iota(jnp.int32, (phases, width), 1)
    left = jnp.zeros((phases, width), F32)
    right = jnp.zeros((phases, width), F32)
    for r in range(ny):
        turned = rows[r] if r == 0 else pltpu.roll(rows[r], 2 * r, 1)
        left = jnp.where((lane >= 2 * r) & (lane < 2 * r + 2), turned, left)
        low = nz - 2 + 2 * r
        right = jnp.where((lane >= low) & (lane < low + 2), turned, right)
    right = pltpu.roll(right, (2 * ny - (nz - 2)) % width, 1)

    labels = labels_ref[...].astype(F32)
    flat = labels.reshape(-1, width)
    pick_lane = lax.broadcasted_iota(jnp.int32, (phases, width), 1)

    def column(z):
        pick = (pick_lane == z).astype(BF16)
        return lax.dot_general(
            pick, flat.astype(BF16), (((1,), (1,)), ((), ())), preferred_element_type=F32
        )

    stage[0] = rows[0]
    stage[1] = rows[1]
    stage[2, 0:2] = labels[:, 0]
    stage[3] = rows[ny - 2]
    stage[4] = rows[ny - 1]
    stage[5, 0:2] = labels[:, 2 * ny - 1]
    stage[6] = left
    stage[7] = column(0)
    stage[8] = right
    stage[9] = column(width - 1)
    out_ref[SLOTS - 1] = left + right

    pl.semaphore_wait(barrier, len(PARTS))
    copies = []
    for n, ((dy, dz), (s0, s1), (d0, d1)) in enumerate(PARTS):
        copy = pltpu.make_async_remote_copy(
            src_ref=stage.at[s0:s1],
            dst_ref=out_ref.at[d0:d1],
            send_sem=send_sem.at[n],
            recv_sem=recv_sem.at[n],
            device_id=other(dy, dz),
            device_id_type=MESH,
        )
        copy.start()
        copies.append(copy)
    for copy in copies:
        copy.wait()


def exact_dot(x, w):
    high = x.astype(BF16)
    low = (x - high.astype(F32)).astype(BF16)
    return jnp.dot(high, w, preferred_element_type=F32) + jnp.dot(low, w, preferred_element_type=F32)


def relax(coarse_ref, labels_ref, mobility_ref, got, main_ref, strip_ref, label_ref, out_ref, p1):
    phases, _, ny, nz = coarse_ref.shape
    width = 2 * nz
    fy = 2 * ny
    shape = (phases, width)
    lane = lax.broadcasted_iota(jnp.int32, shape, 1)
    phase_id = lax.broadcasted_iota(jnp.int32, shape, 0)
    phase_f = phase_id.astype(F32)
    rate = jnp.zeros(shape, F32)
    for p in range(phases):
        rate = jnp.where(phase_id == p, STEP * mobility_ref[p], rate)
    first, last = lane == 0, lane == width - 1
    ends = first | last

    def turn(v, by):
        return pltpu.roll(v, by % width, 1) if by % width else v

    def total(v):
        return jnp.broadcast_to(jnp.sum(v * v, axis=0, keepdims=True), shape)

    def around(c, side):
        return jnp.where(first, side, turn(c, 1)) + jnp.where(last, side, turn(c, -1))

    halo_right = (lane >= nz) & (lane < nz + 2)
    halo_left = lane >= width - 2

    def edge(row, from_left, from_right, left_by=nz, right_by=nz):
        v = jnp.where(halo_right, turn(from_right, right_by), row)
        return jnp.where(halo_left, turn(from_left, left_by), v)

    below = [edge(got[n], got[12 + n], got[10 + n]) for n in range(2)]
    above = [edge(got[3 + n], got[16 + n], got[14 + n]) for n in range(2)]
    x = jnp.swapaxes(coarse_ref[:, 0], 0, 1)
    x = jnp.concatenate([x, jnp.zeros_like(x)], axis=-1)
    top = edge(x[0], got[8], got[6], width - 2 - 2 * ny, nz)
    low = 2 * (ny - 1)
    bottom = edge(x[ny - 1], got[8], got[6], width - 2 - 2 * ny - low, nz - low)
    rows = jnp.concatenate(
        [jnp.stack([*above, top]), x[1 : ny - 1], jnp.stack([bottom, *below])], axis=0
    )
    fine_z = exact_dot(rows.reshape(-1, width), main_ref[...]).reshape(ny + 4, phases, width)

    beside = jnp.where(lane < 2 * ny, got[6], got[8])
    near = (lane < 4) | (lane >= nz - 4) & (lane < nz + 4) | (lane >= width - 4)
    rim = jnp.where(near, above[1], turn(below[0], 8))
    strips = exact_dot(jnp.concatenate([got[SLOTS - 1], beside, rim], axis=1), strip_ref[...])
    outer, side, inner, corner = (strips[:, n * width : (n + 1) * width] for n in range(4))
    near_labels = jnp.concatenate([got[9], got[7]], axis=1).astype(BF16)
    strip_labels = jnp.dot(near_labels, label_ref[...], preferred_element_type=F32)
    up = jnp.where(ends, corner, turn(side, 2))
    down = jnp.where((lane == width - 2) | (lane == width - 3), corner, turn(side, -2))
    side_base = side + rate * (outer + inner + up + down - side * (4.0 + total(side)))
    side1 = [
        side_base + jnp.where(strip_labels[:, n * width : (n + 1) * width] == phase_f, rate, 0.0)
        for n in range(2)
    ]

    def fine_row(y):
        (r0, a), (r1, b) = taps(y)
        v = a * fine_z[r0 + 2] + b * fine_z[r1 + 2]
        return jnp.where(ends, turn(inner, -2 * y), v) if 0 <= y < fy else v

    def label_row(n, y):
        if y < 0:
            row = got[5, n : n + 1]
        elif y >= fy:
            row = got[2, n : n + 1]
        else:
            return jnp.broadcast_to(labels_ref[n, y : y + 1], shape) == phase_id
        return jnp.broadcast_to(row, shape) == phase_f

    def pinned(n, y):
        return jnp.where(label_row(n, y), rate, 0.0)

    prev, cur = fine_row(-2), fine_row(-1)
    for y in range(-1, fy + 1):
        nxt = fine_row(y + 1)
        if y < 0:
            beside_row = corner
        elif y == fy:
            beside_row = turn(corner, 2)
        else:
            beside_row = turn(side, -2 * y)
        base = cur + rate * (prev + nxt + around(cur, beside_row) - cur * (4.0 + total(cur)))
        for n in range(2):
            p1[n, y + 1] = base + pinned(n, y)
        prev, cur = cur, nxt

    for block in range(fy // 8):
        done = [[], []]
        for y in range(8 * block, 8 * block + 8):
            both = [p1[n, y + 1] for n in range(2)]
            for n in range(2):
                c = both[n]
                near = p1[n, y] + p1[n, y + 2] + around(c, turn(side1[n], -2 * y))
                near = near + 2.0 * both[1 - n]
                done[n].append(c + rate * (near - c * (6.0 + total(c))) + pinned(n, y))
        for n in range(2):
            out_ref[:, n, 8 * block : 8 * block + 8] = jnp.swapaxes(jnp.stack(done[n]), 0, 1)


def shards(gy, gz, coarse, labels, mobility):
    phases, planes, ny, nz = coarse.shape
    assert planes == 1 and labels.shape == (2, 2 * ny, 2 * nz) and ny <= nz // 2 and phases == 8
    width = 2 * nz
    vmem = pl.BlockSpec(memory_space=pltpu.VMEM)
    got = pl.pallas_call(
        functools.partial(exchange, gy, gz),
        out_shape=jax.ShapeDtypeStruct((SLOTS, phases, width), F32),
        in_specs=[pl.BlockSpec(memory_space=pltpu.HBM)] * 2,
        out_specs=vmem,
        scratch_shapes=[
            pltpu.VMEM(coarse.shape, F32),
            pltpu.VMEM(labels.shape, jnp.int32),
            pltpu.VMEM((10, phases, width), F32),
            pltpu.SemaphoreType.DMA((len(PARTS),)),
            pltpu.SemaphoreType.DMA((len(PARTS),)),
            pltpu.SemaphoreType.DMA((2,)),
        ],
        compiler_params=pltpu.CompilerParams(
            collective_id=0, has_side_effects=True, vmem_limit_bytes=4 * 2**20
        ),
        name="exchange",
    )(coarse, labels)
    weights = [
        jnp.asarray(w, BF16)
        for w in (main_operator(nz), strip_operator(ny, nz), label_operator(ny, nz))
    ]
    return pl.pallas_call(
        relax,
        out_shape=jax.ShapeDtypeStruct((phases, 2, 2 * ny, width), F32),
        in_specs=[vmem] * 2 + [pl.BlockSpec(memory_space=pltpu.SMEM)] + [vmem] * 4,
        out_specs=vmem,
        scratch_shapes=[pltpu.VMEM((2, 2 * ny + 2, phases, width), F32)],
        compiler_params=pltpu.CompilerParams(vmem_limit_bytes=8 * 2**20),
        name="relax",
    )(coarse, labels, mobility, got, *weights)


def solution(mesh):
    in_specs = (P(None, None, "gy", "gz"), P(None, "gy", "gz"), P())
    out_specs = P(None, None, "gy", "gz")
    fn = functools.partial(shards, mesh.shape["gy"], mesh.shape["gz"])
    return jax.shard_map(fn, mesh=mesh, in_specs=in_specs, out_specs=out_specs, check_vma=False)
```

```python
import functools

import jax
import jax.numpy as jnp
import numpy as np
from jax import lax
from jax.experimental import pallas as pl
from jax.experimental.pallas import tpu as pltpu
from jax.sharding import PartitionSpec as P

STEP = 0.075
MESH = pl.DeviceIdType.MESH
F32 = jnp.float32
BF16 = jnp.bfloat16


def taps(cell):
    i = cell // 2
    return ((i, 0.75), (i + 1 if cell % 2 else i - 1, 0.25))


def col_lane(col, nz):
    return col % (2 * nz)


def main_operator(nz):
    width = 2 * nz
    w = np.zeros((width, width), np.float32)
    for z in range(width):
        for c, a in taps(z):
            w[col_lane(c, nz), z] += a
    return w


def strip_operator(ny, nz):
    width = 2 * nz

    def where(r, c):
        if r == -1:
            return 2 * width + col_lane(c, nz)
        if r == ny:
            return 2 * width + (col_lane(c, nz) + 8) % width
        assert 0 <= r < ny
        if c in (0, 1):
            return 2 * r + c
        if c in (nz - 2, nz - 1):
            return 2 * ny + 2 * r + c - (nz - 2)
        if c in (nz, nz + 1):
            return width + 2 * r + c - nz
        assert c in (-2, -1)
        return width + 2 * ny + 2 * r + c + 2

    w = np.zeros((3 * width, 4 * width), np.float32)

    def put(y, z, out):
        for r, a in taps(y):
            for c, b in taps(z):
                w[where(r, c), out] += a * b

    for y in range(2 * ny):
        left, right = 2 * y, (2 * y - 1) % width
        for block, (zl, zr) in enumerate(((-2, width + 1), (-1, width), (0, width - 1))):
            put(y, zl, block * width + left)
            put(y, zr, block * width + right)
    put(-1, -1, 3 * width)
    put(-1, width, 3 * width + width - 1)
    put(2 * ny, -1, 3 * width + width - 2)
    put(2 * ny, width, 3 * width + width - 3)
    return w


def label_operator(ny, nz):
    width = 2 * nz
    w = np.zeros((2 * width, 2 * width), np.float32)
    for x in range(2):
        for y in range(2 * ny):
            w[x * 2 * ny + y, x * width + 2 * y] = 1
            w[width + x * 2 * ny + y, x * width + (2 * y - 1) % width] = 1
    return w


PARTS = (
    ((-1, 0), (0, 3), (0, 3)),
    ((1, 0), (3, 6), (3, 6)),
    ((0, -1), (6, 8), (6, 8)),
    ((0, 1), (8, 10), (8, 10)),
    ((-1, -1), (0, 2), (10, 12)),
    ((-1, 1), (0, 2), (12, 14)),
    ((1, -1), (3, 5), (14, 16)),
    ((1, 1), (3, 5), (16, 18)),
)
SLOTS = 21


def wide(x):
    return jnp.concatenate([x, jnp.zeros_like(x)], axis=-1)


def exact_dot(x, w):
    high = x.astype(BF16)
    low = (x - high.astype(F32)).astype(BF16)
    return jnp.dot(high, w, preferred_element_type=F32) + jnp.dot(low, w, preferred_element_type=F32)


def exchange(gy, gz, *refs):
    mobility_ref, sources, refs = refs[0], refs[1:6], refs[6:]
    got, fine_ref, rate_ref, labels_ref, main_ref, strip_ref, label_ref = refs[:7]
    coarse_ref, stage, send_sem, recv_sem, load_sem = refs[7:]
    me_y, me_z = lax.axis_index("gy"), lax.axis_index("gz")

    def other(dy, dz):
        return (lax.rem(me_y + dy + gy, gy), lax.rem(me_z + dz + gz, gz))

    barrier = pltpu.get_barrier_semaphore()
    for (dy, dz), _, _ in PARTS:
        pl.semaphore_signal(barrier, inc=1, device_id=other(dy, dz), device_id_type=MESH)
    targets = (coarse_ref, labels_ref, main_ref, strip_ref, label_ref)
    loads = [
        pltpu.make_async_copy(source, target, load_sem.at[n])
        for n, (source, target) in enumerate(zip(sources, targets))
    ]
    for load in loads:
        load.start()

    phases, _, ny, nz = coarse_ref.shape
    width = 2 * nz
    lane = lax.broadcasted_iota(jnp.int32, (phases, width), 1)
    loads[0].wait()
    x = wide(jnp.swapaxes(coarse_ref[:, 0], 0, 1))
    rows = [x[r] for r in range(ny)]
    stage[0] = rows[0]
    stage[1] = rows[1]
    stage[3] = rows[ny - 2]
    stage[4] = rows[ny - 1]
    left = jnp.zeros((phases, width), F32)
    right = jnp.zeros((phases, width), F32)
    for r in range(ny):
        turned = rows[r] if r == 0 else pltpu.roll(rows[r], 2 * r, 1)
        left = jnp.where((lane >= 2 * r) & (lane < 2 * r + 2), turned, left)
        low = nz - 2 + 2 * r
        right = jnp.where((lane >= low) & (lane < low + 2), turned, right)
    right = pltpu.roll(right, (2 * ny - (nz - 2)) % width, 1)
    stage[6] = left
    stage[8] = right
    got[SLOTS - 3] = rows[0]
    got[SLOTS - 2] = rows[ny - 1]
    got[SLOTS - 1] = left + right

    loads[1].wait()
    flat = labels_ref[...].reshape(-1, width).astype(F32).astype(BF16)

    def column(z):
        pick = (lane == z).astype(BF16)
        return lax.dot_general(
            pick, flat, (((1,), (1,)), ((), ())), preferred_element_type=F32
        )

    stage[2, 0:2] = labels_ref[:, 0].astype(F32)
    stage[5, 0:2] = labels_ref[:, 2 * ny - 1].astype(F32)
    stage[7] = column(0)
    stage[9] = column(width - 1)

    pl.semaphore_wait(barrier, len(PARTS))
    copies = []
    for n, ((dy, dz), (s0, s1), (d0, d1)) in enumerate(PARTS):
        copy = pltpu.make_async_remote_copy(
            src_ref=stage.at[s0:s1],
            dst_ref=got.at[d0:d1],
            send_sem=send_sem.at[n],
            recv_sem=recv_sem.at[n],
            device_id=other(dy, dz),
            device_id_type=MESH,
        )
        copy.start()
        copies.append(copy)

    phase_id = lax.broadcasted_iota(jnp.int32, (phases, width), 0)
    rate = jnp.zeros((phases, width), F32)
    for p in range(phases):
        rate = jnp.where(phase_id == p, STEP * mobility_ref[p], rate)
    rate_ref[...] = rate
    loads[2].wait()
    fine_ref[...] = exact_dot(x.reshape(-1, width), main_ref[...]).reshape(fine_ref.shape)
    for load in loads[3:]:
        load.wait()
    for copy in copies:
        copy.wait()


def relax(
    got, own, rate_ref, labels_ref, main_ref, strip_ref, label_ref, out_hbm, p1, out_ref, out_sem
):
    ny, phases, width = own.shape
    nz, fy = width // 2, 2 * ny
    shape = (phases, width)
    lane = lax.broadcasted_iota(jnp.int32, shape, 1)
    phase_id = lax.broadcasted_iota(jnp.int32, shape, 0)
    phase_f = phase_id.astype(F32)
    rate = rate_ref[...]
    first, last = lane == 0, lane == width - 1
    ends = first | last

    def turn(v, by):
        return pltpu.roll(v, by % width, 1) if by % width else v

    def total(v):
        return jnp.broadcast_to(jnp.sum(v * v, axis=0, keepdims=True), shape)

    def around(c, side):
        return jnp.where(first, side, turn(c, 1)) + jnp.where(last, side, turn(c, -1))

    halo_right = (lane >= nz) & (lane < nz + 2)
    halo_left = lane >= width - 2

    def edge(row, from_left, from_right, left_by=nz, right_by=nz):
        v = jnp.where(halo_right, turn(from_right, right_by), row)
        return jnp.where(halo_left, turn(from_left, left_by), v)

    below = [edge(got[n], got[12 + n], got[10 + n]) for n in range(2)]
    above = [edge(got[3 + n], got[16 + n], got[14 + n]) for n in range(2)]
    low = 2 * (ny - 1)
    top = edge(got[SLOTS - 3], got[8], got[6], width - 2 - 2 * ny, nz)
    bottom = edge(got[SLOTS - 2], got[8], got[6], width - 2 - 2 * ny - low, nz - low)
    rim_rows = jnp.concatenate([*above, top, bottom, *below], axis=0)
    rim_fine = exact_dot(rim_rows, main_ref[...])
    rim_fine = [rim_fine[n * phases : (n + 1) * phases] for n in range(6)]
    fine_z = [*rim_fine[:3], *(own[r] for r in range(1, ny - 1)), *rim_fine[3:]]

    beside = jnp.where(lane < 2 * ny, got[6], got[8])
    near = (lane < 4) | (lane >= nz - 4) & (lane < nz + 4) | (lane >= width - 4)
    rim = jnp.where(near, above[1], turn(below[0], 8))
    strips = exact_dot(jnp.concatenate([got[SLOTS - 1], beside, rim], axis=1), strip_ref[...])
    outer, side, inner, corner = (strips[:, n * width : (n + 1) * width] for n in range(4))
    near_labels = jnp.concatenate([got[9], got[7]], axis=1).astype(BF16)
    strip_labels = jnp.dot(near_labels, label_ref[...], preferred_element_type=F32)
    up = jnp.where(ends, corner, turn(side, 2))
    down = jnp.where((lane == width - 2) | (lane == width - 3), corner, turn(side, -2))
    side_base = side + rate * (outer + inner + up + down - side * (4.0 + total(side)))
    side1 = [
        side_base + jnp.where(strip_labels[:, n * width : (n + 1) * width] == phase_f, rate, 0.0)
        for n in range(2)
    ]

    def fine_row(y):
        (r0, a), (r1, b) = taps(y)
        v = a * fine_z[r0 + 2] + b * fine_z[r1 + 2]
        return jnp.where(ends, turn(inner, -2 * y), v) if 0 <= y < fy else v

    def label_row(n, y):
        if y < 0:
            row = got[5, n : n + 1]
        elif y >= fy:
            row = got[2, n : n + 1]
        else:
            return jnp.broadcast_to(labels_ref[n, y : y + 1], shape) == phase_id
        return jnp.broadcast_to(row, shape) == phase_f

    def pinned(n, y):
        return jnp.where(label_row(n, y), rate, 0.0)

    def first_step(y, prev, cur, nxt):
        if y < 0:
            beside_row = corner
        elif y == fy:
            beside_row = turn(corner, 2)
        else:
            beside_row = turn(side, -2 * y)
        base = cur + rate * (prev + nxt + around(cur, beside_row) - cur * (4.0 + total(cur)))
        for n in range(2):
            p1[n, y + 1] = base + pinned(n, y)

    def second_step(block):
        done = [[], []]
        for y in range(8 * block, 8 * block + 8):
            both = [p1[n, y + 1] for n in range(2)]
            for n in range(2):
                c = both[n]
                near = p1[n, y] + p1[n, y + 2] + around(c, turn(side1[n], -2 * y))
                near = near + 2.0 * both[1 - n]
                done[n].append(c + rate * (near - c * (6.0 + total(c))) + pinned(n, y))
        for n in range(2):
            out_ref[block, :, n] = jnp.swapaxes(jnp.stack(done[n]), 0, 1)
        copy = pltpu.make_async_copy(
            out_ref.at[block], out_hbm.at[:, :, pl.ds(8 * block, 8)], out_sem.at[block]
        )
        copy.start()
        return copy

    copies = []
    prev, cur = fine_row(-2), fine_row(-1)
    for y in range(-1, fy + 1):
        nxt = fine_row(y + 1)
        first_step(y, prev, cur, nxt)
        prev, cur = cur, nxt
        if y > 0 and y % 8 == 0:
            copies.append(second_step(y // 8 - 1))
    for copy in copies:
        copy.wait()


def shards(gy, gz, coarse, labels, mobility):
    phases, planes, ny, nz = coarse.shape
    assert planes == 1 and labels.shape == (2, 2 * ny, 2 * nz) and ny <= nz // 2 and phases == 8
    width = 2 * nz
    vmem = pl.BlockSpec(memory_space=pltpu.VMEM)
    hbm = pl.BlockSpec(memory_space=pltpu.HBM)
    weights = [
        jnp.asarray(w, BF16)
        for w in (main_operator(nz), strip_operator(ny, nz), label_operator(ny, nz))
    ]
    sources = [pltpu.with_memory_space_constraint(v, pltpu.HBM) for v in (coarse, labels, *weights)]
    shared = [
        pltpu.VMEM((SLOTS, phases, width), F32),
        pltpu.VMEM((ny, phases, width), F32),
        pltpu.VMEM((phases, width), F32),
        *(pltpu.VMEM(v.shape, v.dtype) for v in (labels, *weights)),
    ]
    parts = pl.pallas_call(
        functools.partial(exchange, gy, gz),
        out_shape=shared,
        in_specs=[pl.BlockSpec(memory_space=pltpu.SMEM)] + [hbm] * len(sources),
        out_specs=[vmem] * len(shared),
        scratch_shapes=[
            pltpu.VMEM(coarse.shape, F32),
            pltpu.VMEM((10, phases, width), F32),
            pltpu.SemaphoreType.DMA((len(PARTS),)),
            pltpu.SemaphoreType.DMA((len(PARTS),)),
            pltpu.SemaphoreType.DMA((len(sources),)),
        ],
        compiler_params=pltpu.CompilerParams(
            collective_id=0, has_side_effects=True, vmem_limit_bytes=8 * 2**20
        ),
        name="exchange",
    )(mobility, *sources)
    return pl.pallas_call(
        relax,
        out_shape=jax.ShapeDtypeStruct((phases, 2, 2 * ny, width), F32),
        in_specs=[vmem] * len(shared),
        out_specs=hbm,
        scratch_shapes=[
            pltpu.VMEM((2, 2 * ny + 2, phases, width), F32),
            pltpu.VMEM((2 * ny // 8, phases, 2, 8, width), F32),
            pltpu.SemaphoreType.DMA((2 * ny // 8,)),
        ],
        compiler_params=pltpu.CompilerParams(vmem_limit_bytes=8 * 2**20),
        name="relax",
    )(*parts)


def solution(mesh):
    in_specs = (P(None, None, "gy", "gz"), P(None, "gy", "gz"), P())
    out_specs = P(None, None, "gy", "gz")
    fn = functools.partial(shards, mesh.shape["gy"], mesh.shape["gz"])
    return jax.shard_map(fn, mesh=mesh, in_specs=in_specs, out_specs=out_specs, check_vma=False)
```

```python
import functools

import jax
import jax.numpy as jnp
import numpy as np
from jax import lax
from jax.experimental import pallas as pl
from jax.experimental.pallas import tpu as pltpu
from jax.sharding import PartitionSpec as P

STEP = 0.075
MESH = pl.DeviceIdType.MESH
F32 = jnp.float32
BF16 = jnp.bfloat16


def taps(cell):
    i = cell // 2
    return ((i, 0.75), (i + 1 if cell % 2 else i - 1, 0.25))


def col_lane(col, nz):
    return col % (2 * nz)


def main_operator(nz):
    width = 2 * nz
    w = np.zeros((width, width), np.float32)
    for z in range(width):
        for c, a in taps(z):
            w[col_lane(c, nz), z] += a
    return w


def strip_operator(ny, nz):
    width = 2 * nz

    def where(r, c):
        if r == -1:
            return 2 * width + col_lane(c, nz)
        if r == ny:
            return 2 * width + (col_lane(c, nz) + 8) % width
        assert 0 <= r < ny
        if c in (0, 1):
            return 2 * r + c
        if c in (nz - 2, nz - 1):
            return 2 * ny + 2 * r + c - (nz - 2)
        if c in (nz, nz + 1):
            return width + 2 * r + c - nz
        assert c in (-2, -1)
        return width + 2 * ny + 2 * r + c + 2

    w = np.zeros((3 * width, 4 * width), np.float32)

    def put(y, z, out):
        for r, a in taps(y):
            for c, b in taps(z):
                w[where(r, c), out] += a * b

    for y in range(2 * ny):
        left, right = 2 * y, (2 * y - 1) % width
        for block, (zl, zr) in enumerate(((-2, width + 1), (-1, width), (0, width - 1))):
            put(y, zl, block * width + left)
            put(y, zr, block * width + right)
    put(-1, -1, 3 * width)
    put(-1, width, 3 * width + width - 1)
    put(2 * ny, -1, 3 * width + width - 2)
    put(2 * ny, width, 3 * width + width - 3)
    return w


def label_operator(ny, nz):
    width = 2 * nz
    w = np.zeros((2 * width, 2 * width), np.float32)
    for x in range(2):
        for y in range(2 * ny):
            w[x * 2 * ny + y, x * width + 2 * y] = 1
            w[width + x * 2 * ny + y, x * width + (2 * y - 1) % width] = 1
    return w


PARTS = (
    ((-1, 0), (0, 3), (0, 3)),
    ((1, 0), (3, 6), (3, 6)),
    ((0, -1), (6, 8), (6, 8)),
    ((0, 1), (8, 10), (8, 10)),
    ((-1, -1), (0, 2), (10, 12)),
    ((-1, 1), (0, 2), (12, 14)),
    ((1, -1), (3, 5), (14, 16)),
    ((1, 1), (3, 5), (16, 18)),
)
SLOTS = 20


def wide(x):
    return jnp.concatenate([x, jnp.zeros_like(x)], axis=-1)


def exact_dot(x, w):
    high = x.astype(BF16).astype(F32)
    both = jnp.concatenate([high, x - high], axis=0).astype(BF16)
    product = jnp.dot(both, w, preferred_element_type=F32)
    return product[: x.shape[0]] + product[x.shape[0] :]


def exchange(gy, gz, *refs):
    sources, refs = refs[:6], refs[6:]
    got, fine_ref, pin_ref, rate_ref, strips_ref, main_ref, strip_ref, label_ref = refs[:8]
    mobility_ref, labels_ref, coarse_ref, stage, send_sem, recv_sem, load_sem = refs[8:]
    me_y, me_z = lax.axis_index("gy"), lax.axis_index("gz")

    def other(dy, dz):
        return (lax.rem(me_y + dy + gy, gy), lax.rem(me_z + dz + gz, gz))

    barrier = pltpu.get_barrier_semaphore()
    for (dy, dz), _, _ in PARTS:
        pl.semaphore_signal(barrier, inc=1, device_id=other(dy, dz), device_id_type=MESH)
    targets = (coarse_ref, labels_ref, mobility_ref, main_ref, strip_ref, label_ref)
    loads = [
        pltpu.make_async_copy(source, target, load_sem.at[n])
        for n, (source, target) in enumerate(zip(sources, targets))
    ]
    for load in loads:
        load.start()

    phases, _, ny, nz = coarse_ref.shape
    width = 2 * nz
    lane = lax.broadcasted_iota(jnp.int32, (phases, width), 1)
    loads[0].wait()
    x = wide(jnp.swapaxes(coarse_ref[:, 0], 0, 1))
    rows = [x[r] for r in range(ny)]
    stage[0] = rows[0]
    stage[1] = rows[1]
    stage[3] = rows[ny - 2]
    stage[4] = rows[ny - 1]
    left = jnp.zeros((phases, width), F32)
    right = jnp.zeros((phases, width), F32)
    for r in range(ny):
        turned = rows[r] if r == 0 else pltpu.roll(rows[r], 2 * r, 1)
        left = jnp.where((lane >= 2 * r) & (lane < 2 * r + 2), turned, left)
        low = nz - 2 + 2 * r
        right = jnp.where((lane >= low) & (lane < low + 2), turned, right)
    right = pltpu.roll(right, (2 * ny - (nz - 2)) % width, 1)
    stage[6] = left
    stage[8] = right
    got[SLOTS - 2] = rows[0]
    got[SLOTS - 1] = rows[ny - 1]

    loads[1].wait()
    flat = labels_ref[...].reshape(-1, width).astype(F32).astype(BF16)

    def column(z):
        pick = (lane == z).astype(BF16)
        return lax.dot_general(
            pick, flat, (((1,), (1,)), ((), ())), preferred_element_type=F32
        )

    stage[2, 0:2] = labels_ref[:, 0].astype(F32)
    stage[5, 0:2] = labels_ref[:, 2 * ny - 1].astype(F32)
    stage[7] = column(0)
    stage[9] = column(width - 1)

    pl.semaphore_wait(barrier, len(PARTS))
    copies = []
    for n, ((dy, dz), (s0, s1), (d0, d1)) in enumerate(PARTS):
        copy = pltpu.make_async_remote_copy(
            src_ref=stage.at[s0:s1],
            dst_ref=got.at[d0:d1],
            send_sem=send_sem.at[n],
            recv_sem=recv_sem.at[n],
            device_id=other(dy, dz),
            device_id_type=MESH,
        )
        copy.start()
        copies.append(copy)

    phase_id = lax.broadcasted_iota(jnp.int32, (phases, width), 0)
    rate = jnp.zeros((phases, width), F32)
    loads[2].wait()
    for p in range(phases):
        rate = jnp.where(phase_id == p, STEP * mobility_ref[p], rate)
    rate_ref[...] = rate
    loads[3].wait()
    fine_z = exact_dot(x.reshape(-1, width), main_ref[...]).reshape(ny, phases, width)
    for y in range(1, 2 * ny - 1):
        (r0, a), (r1, b) = taps(y)
        fine_ref[y] = a * fine_z[r0] + b * fine_z[r1]
    for n in range(2):
        for y in range(2 * ny):
            label = jnp.broadcast_to(labels_ref[n, y : y + 1], rate.shape)
            pin_ref[n, y] = jnp.where(label == phase_id, rate, 0.0)
    loads[4].wait()
    strips_ref[...] = exact_dot(left + right, strip_ref[:width])
    loads[5].wait()
    for copy in copies:
        copy.wait()


def relax(
    got, fine, pin, rate_ref, strips_ref, main_ref, strip_ref, label_ref, *rest
):
    out_hbm, p1, out_ref, out_sem = rest
    fy, phases, width = fine.shape
    ny, nz = fy // 2, width // 2
    shape = (phases, width)
    lane = lax.broadcasted_iota(jnp.int32, shape, 1)
    phase_id = lax.broadcasted_iota(jnp.int32, shape, 0)
    phase_f = phase_id.astype(F32)
    rate = rate_ref[...]
    first, last = lane == 0, lane == width - 1
    ends = first | last

    def turn(v, by):
        return pltpu.roll(v, by % width, 1) if by % width else v

    def total(v):
        return jnp.broadcast_to(jnp.sum(v * v, axis=0, keepdims=True), shape)

    def around(c, side):
        return jnp.where(first, side, turn(c, 1)) + jnp.where(last, side, turn(c, -1))

    halo_right = (lane >= nz) & (lane < nz + 2)
    halo_left = lane >= width - 2

    def edge(row, from_left, from_right, left_by=nz, right_by=nz):
        v = jnp.where(halo_right, turn(from_right, right_by), row)
        return jnp.where(halo_left, turn(from_left, left_by), v)

    below = [edge(got[n], got[12 + n], got[10 + n]) for n in range(2)]
    above = [edge(got[3 + n], got[16 + n], got[14 + n]) for n in range(2)]
    low = 2 * (ny - 1)
    top = edge(got[SLOTS - 2], got[8], got[6], width - 2 - 2 * ny, nz)
    bottom = edge(got[SLOTS - 1], got[8], got[6], width - 2 - 2 * ny - low, nz - low)
    rim_rows = jnp.concatenate([*above, top, bottom, *below], axis=0)
    rim_fine = exact_dot(rim_rows, main_ref[...])
    rim_fine = [rim_fine[n * phases : (n + 1) * phases] for n in range(6)]
    at_rim = dict(zip((-2, -1, 0, ny - 1, ny, ny + 1), rim_fine))

    beside = jnp.where(lane < 2 * ny, got[6], got[8])
    near = (lane < 4) | (lane >= nz - 4) & (lane < nz + 4) | (lane >= width - 4)
    rim = jnp.where(near, above[1], turn(below[0], 8))
    strips = exact_dot(jnp.concatenate([beside, rim], axis=1), strip_ref[width:])
    strips = strips + strips_ref[...]
    outer, side, inner, corner = (strips[:, n * width : (n + 1) * width] for n in range(4))
    near_labels = jnp.concatenate([got[9], got[7]], axis=1).astype(BF16)
    strip_labels = jnp.dot(near_labels, label_ref[...], preferred_element_type=F32)
    up = jnp.where(ends, corner, turn(side, 2))
    down = jnp.where((lane == width - 2) | (lane == width - 3), corner, turn(side, -2))
    side_base = side + rate * (outer + inner + up + down - side * (4.0 + total(side)))
    side1 = [
        side_base + jnp.where(strip_labels[:, n * width : (n + 1) * width] == phase_f, rate, 0.0)
        for n in range(2)
    ]

    def fine_row(y):
        if 0 < y < fy - 1:
            v = fine[y]
        else:
            (r0, a), (r1, b) = taps(y)
            v = a * at_rim[r0] + b * at_rim[r1]
        return jnp.where(ends, turn(inner, -2 * y), v) if 0 <= y < fy else v

    def pinned(n, y):
        if 0 <= y < fy:
            return pin[n, y]
        row = got[5, n : n + 1] if y < 0 else got[2, n : n + 1]
        return jnp.where(jnp.broadcast_to(row, shape) == phase_f, rate, 0.0)

    def first_step(y, prev, cur, nxt):
        if y < 0:
            beside_row = corner
        elif y == fy:
            beside_row = turn(corner, 2)
        else:
            beside_row = turn(side, -2 * y)
        base = cur + rate * (prev + nxt + around(cur, beside_row) - cur * (4.0 + total(cur)))
        for n in range(2):
            p1[n, y + 1] = base + pinned(n, y)

    def second_step(block):
        done = [[], []]
        for y in range(8 * block, 8 * block + 8):
            both = [p1[n, y + 1] for n in range(2)]
            for n in range(2):
                c = both[n]
                near = p1[n, y] + p1[n, y + 2] + around(c, turn(side1[n], -2 * y))
                near = near + 2.0 * both[1 - n]
                done[n].append(c + rate * (near - c * (6.0 + total(c))) + pinned(n, y))
        for n in range(2):
            out_ref[block, :, n] = jnp.swapaxes(jnp.stack(done[n]), 0, 1)
        copy = pltpu.make_async_copy(
            out_ref.at[block], out_hbm.at[:, :, pl.ds(8 * block, 8)], out_sem.at[block]
        )
        copy.start()
        return copy

    copies = []
    prev, cur = fine_row(-2), fine_row(-1)
    for y in range(-1, fy + 1):
        nxt = fine_row(y + 1)
        first_step(y, prev, cur, nxt)
        prev, cur = cur, nxt
        if y > 0 and y % 8 == 0:
            copies.append(second_step(y // 8 - 1))
    for copy in copies:
        copy.wait()


def shards(gy, gz, coarse, labels, mobility):
    phases, planes, ny, nz = coarse.shape
    assert planes == 1 and labels.shape == (2, 2 * ny, 2 * nz) and ny <= nz // 2 and phases == 8
    width = 2 * nz
    vmem = pl.BlockSpec(memory_space=pltpu.VMEM)
    hbm = pl.BlockSpec(memory_space=pltpu.HBM)
    weights = [
        jnp.asarray(w, BF16)
        for w in (main_operator(nz), strip_operator(ny, nz), label_operator(ny, nz))
    ]
    sources = [pltpu.with_memory_space_constraint(v, pltpu.HBM) for v in (coarse, labels, mobility, *weights)]
    shared = [
        pltpu.VMEM((SLOTS, phases, width), F32),
        pltpu.VMEM((2 * ny, phases, width), F32),
        pltpu.VMEM((2, 2 * ny, phases, width), F32),
        pltpu.VMEM((phases, width), F32),
        pltpu.VMEM((phases, 4 * width), F32),
        *(pltpu.VMEM(v.shape, v.dtype) for v in weights),
    ]
    parts = pl.pallas_call(
        functools.partial(exchange, gy, gz),
        out_shape=shared,
        in_specs=[hbm] * len(sources),
        out_specs=[vmem] * len(shared),
        scratch_shapes=[
            pltpu.SMEM(mobility.shape, F32),
            pltpu.VMEM(labels.shape, jnp.int32),
            pltpu.VMEM(coarse.shape, F32),
            pltpu.VMEM((10, phases, width), F32),
            pltpu.SemaphoreType.DMA((len(PARTS),)),
            pltpu.SemaphoreType.DMA((len(PARTS),)),
            pltpu.SemaphoreType.DMA((len(sources),)),
        ],
        compiler_params=pltpu.CompilerParams(
            collective_id=0, has_side_effects=True, vmem_limit_bytes=8 * 2**20
        ),
        name="exchange",
    )(*sources)
    return pl.pallas_call(
        relax,
        out_shape=jax.ShapeDtypeStruct((phases, 2, 2 * ny, width), F32),
        in_specs=[vmem] * len(shared),
        out_specs=hbm,
        scratch_shapes=[
            pltpu.VMEM((2, 2 * ny + 2, phases, width), F32),
            pltpu.VMEM((2 * ny // 8, phases, 2, 8, width), F32),
            pltpu.SemaphoreType.DMA((2 * ny // 8,)),
        ],
        compiler_params=pltpu.CompilerParams(vmem_limit_bytes=8 * 2**20),
        name="relax",
    )(*parts)


def solution(mesh):
    in_specs = (P(None, None, "gy", "gz"), P(None, "gy", "gz"), P())
    out_specs = P(None, None, "gy", "gz")
    fn = functools.partial(shards, mesh.shape["gy"], mesh.shape["gz"])
    return jax.shard_map(fn, mesh=mesh, in_specs=in_specs, out_specs=out_specs, check_vma=False)
```

```python
import functools

import jax
import jax.numpy as jnp
import numpy as np
from jax import lax
from jax.experimental import pallas as pl
from jax.experimental.pallas import tpu as pltpu
from jax.sharding import PartitionSpec as P

STEP = 0.075
MESH = pl.DeviceIdType.MESH
F32 = jnp.float32
BF16 = jnp.bfloat16


def taps(cell):
    i = cell // 2
    return ((i, 0.75), (i + 1 if cell % 2 else i - 1, 0.25))


def col_lane(col, nz):
    return col % (2 * nz)


def main_operator(nz):
    width = 2 * nz
    w = np.zeros((width, width), np.float32)
    for z in range(width):
        for c, a in taps(z):
            w[col_lane(c, nz), z] += a
    return w


def strip_operator(ny, nz):
    width = 2 * nz

    def where(r, c):
        if r == -1:
            return 2 * width + col_lane(c, nz)
        if r == ny:
            return 2 * width + (col_lane(c, nz) + 8) % width
        assert 0 <= r < ny
        if c in (0, 1):
            return 2 * r + c
        if c in (nz - 2, nz - 1):
            return 2 * ny + 2 * r + c - (nz - 2)
        if c in (nz, nz + 1):
            return width + 2 * r + c - nz
        assert c in (-2, -1)
        return width + 2 * ny + 2 * r + c + 2

    w = np.zeros((3 * width, 4 * width), np.float32)

    def put(y, z, out):
        for r, a in taps(y):
            for c, b in taps(z):
                w[where(r, c), out] += a * b

    for y in range(2 * ny):
        left, right = 2 * y, (2 * y - 1) % width
        for block, (zl, zr) in enumerate(((-2, width + 1), (-1, width), (0, width - 1))):
            put(y, zl, block * width + left)
            put(y, zr, block * width + right)
    put(-1, -1, 3 * width)
    put(-1, width, 3 * width + width - 1)
    put(2 * ny, -1, 3 * width + width - 2)
    put(2 * ny, width, 3 * width + width - 3)
    return w


def label_operator(ny, nz):
    width = 2 * nz
    w = np.zeros((2 * width, 2 * width), np.float32)
    for x in range(2):
        for y in range(2 * ny):
            w[x * 2 * ny + y, x * width + 2 * y] = 1
            w[width + x * 2 * ny + y, x * width + (2 * y - 1) % width] = 1
    return w


PARTS = (
    ((-1, 0), (0, 3), (0, 3)),
    ((1, 0), (3, 6), (3, 6)),
    ((0, -1), (6, 8), (6, 8)),
    ((0, 1), (8, 10), (8, 10)),
    ((-1, -1), (0, 2), (10, 12)),
    ((-1, 1), (0, 2), (12, 14)),
    ((1, -1), (3, 5), (14, 16)),
    ((1, 1), (3, 5), (16, 18)),
)
SLOTS = 20


def wide(x):
    return jnp.concatenate([x, jnp.zeros_like(x)], axis=-1)


def exact_dot(x, w):
    high = x.astype(BF16).astype(F32)
    both = jnp.concatenate([high, x - high], axis=0).astype(BF16)
    product = jnp.dot(both, w, preferred_element_type=F32)
    return product[: x.shape[0]] + product[x.shape[0] :]


def exchange(gy, gz, *refs):
    sources, refs = refs[:6], refs[6:]
    got, fine_ref, pin_ref, rate_ref, strips_ref, beside_ref, ones_ref = refs[:7]
    main_ref, strip_ref, label_ref = refs[7:10]
    mobility_ref, labels_ref, coarse_ref, stage, send_sem, recv_sem, load_sem = refs[10:]
    me_y, me_z = lax.axis_index("gy"), lax.axis_index("gz")

    def other(dy, dz):
        return (lax.rem(me_y + dy + gy, gy), lax.rem(me_z + dz + gz, gz))

    barrier = pltpu.get_barrier_semaphore()
    for (dy, dz), _, _ in PARTS:
        pl.semaphore_signal(barrier, inc=1, device_id=other(dy, dz), device_id_type=MESH)
    targets = (coarse_ref, labels_ref, mobility_ref, main_ref, strip_ref, label_ref)
    loads = [
        pltpu.make_async_copy(source, target, load_sem.at[n])
        for n, (source, target) in enumerate(zip(sources, targets))
    ]
    for load in loads:
        load.start()

    phases, _, ny, nz = coarse_ref.shape
    width = 2 * nz
    lane = lax.broadcasted_iota(jnp.int32, (phases, width), 1)
    loads[0].wait()
    x = wide(jnp.swapaxes(coarse_ref[:, 0], 0, 1))
    rows = [x[r] for r in range(ny)]
    stage[0] = rows[0]
    stage[1] = rows[1]
    stage[3] = rows[ny - 2]
    stage[4] = rows[ny - 1]
    left = jnp.zeros((phases, width), F32)
    right = jnp.zeros((phases, width), F32)
    for r in range(ny):
        turned = rows[r] if r == 0 else pltpu.roll(rows[r], 2 * r, 1)
        left = jnp.where((lane >= 2 * r) & (lane < 2 * r + 2), turned, left)
        low = nz - 2 + 2 * r
        right = jnp.where((lane >= low) & (lane < low + 2), turned, right)
    right = pltpu.roll(right, (2 * ny - (nz - 2)) % width, 1)
    stage[6] = left
    stage[8] = right
    got[SLOTS - 2] = rows[0]
    got[SLOTS - 1] = rows[ny - 1]

    loads[1].wait()
    flat = labels_ref[...].reshape(-1, width).astype(F32).astype(BF16)

    def column(z):
        pick = (lane == z).astype(BF16)
        return lax.dot_general(
            pick, flat, (((1,), (1,)), ((), ())), preferred_element_type=F32
        )

    stage[2, 0:2] = labels_ref[:, 0].astype(F32)
    stage[5, 0:2] = labels_ref[:, 2 * ny - 1].astype(F32)
    stage[7] = column(0)
    stage[9] = column(width - 1)

    pl.semaphore_wait(barrier, len(PARTS))
    copies = []
    for n, ((dy, dz), (s0, s1), (d0, d1)) in enumerate(PARTS):
        copy = pltpu.make_async_remote_copy(
            src_ref=stage.at[s0:s1],
            dst_ref=got.at[d0:d1],
            send_sem=send_sem.at[n],
            recv_sem=recv_sem.at[n],
            device_id=other(dy, dz),
            device_id_type=MESH,
        )
        copy.start()
        copies.append(copy)

    phase_id = lax.broadcasted_iota(jnp.int32, (phases, width), 0)
    rate = jnp.zeros((phases, width), F32)
    loads[2].wait()
    for p in range(phases):
        rate = jnp.where(phase_id == p, STEP * mobility_ref[p], rate)
    rate_ref[...] = rate
    loads[3].wait()
    fine_z = exact_dot(x.reshape(-1, width), main_ref[...]).reshape(ny, phases, width)
    for y in range(1, 2 * ny - 1):
        (r0, a), (r1, b) = taps(y)
        fine_ref[y] = a * fine_z[r0] + b * fine_z[r1]
    for n in range(2):
        for y in range(2 * ny):
            label = jnp.broadcast_to(labels_ref[n, y : y + 1], rate.shape)
            pin_ref[n, y] = jnp.where(label == phase_id, rate, 0.0)
    row = lax.broadcasted_iota(jnp.int32, beside_ref.shape, 0) % width
    column_id = lax.broadcasted_iota(jnp.int32, beside_ref.shape, 1)
    beside_ref[...] = (jnp.abs(row - column_id) == 1).astype(F32).astype(BF16)
    row = lax.broadcasted_iota(jnp.int32, ones_ref.shape, 0)
    column_id = lax.broadcasted_iota(jnp.int32, ones_ref.shape, 1) % (8 * phases)
    ones_ref[...] = (row // phases == column_id // phases).astype(F32).astype(BF16)
    loads[4].wait()
    strips_ref[...] = exact_dot(left + right, strip_ref[:width])
    loads[5].wait()
    for copy in copies:
        copy.wait()


def relax(
    got, fine, pin, rate_ref, strips_ref, beside_ref, ones_ref, main_ref, strip_ref, label_ref, *rest
):
    out_hbm, p1, out_ref, out_sem = rest
    fy, phases, width = fine.shape
    ny, nz = fy // 2, width // 2
    shape = (phases, width)
    lane = lax.broadcasted_iota(jnp.int32, shape, 1)
    phase_id = lax.broadcasted_iota(jnp.int32, shape, 0)
    phase_f = phase_id.astype(F32)
    rate = rate_ref[...]
    first, last = lane == 0, lane == width - 1
    ends = first | last

    def turn(v, by):
        return pltpu.roll(v, by % width, 1) if by % width else v

    def total(v):
        return jnp.broadcast_to(jnp.sum(v * v, axis=0, keepdims=True), shape)

    def around(c, side):
        return jnp.where(first, side, turn(c, 1)) + jnp.where(last, side, turn(c, -1))

    halo_right = (lane >= nz) & (lane < nz + 2)
    halo_left = lane >= width - 2

    def edge(row, from_left, from_right, left_by=nz, right_by=nz):
        v = jnp.where(halo_right, turn(from_right, right_by), row)
        return jnp.where(halo_left, turn(from_left, left_by), v)

    below = [edge(got[n], got[12 + n], got[10 + n]) for n in range(2)]
    above = [edge(got[3 + n], got[16 + n], got[14 + n]) for n in range(2)]
    low = 2 * (ny - 1)
    top = edge(got[SLOTS - 2], got[8], got[6], width - 2 - 2 * ny, nz)
    bottom = edge(got[SLOTS - 1], got[8], got[6], width - 2 - 2 * ny - low, nz - low)
    rim_rows = jnp.concatenate([*above, top, bottom, *below], axis=0)
    rim_fine = exact_dot(rim_rows, main_ref[...])
    rim_fine = [rim_fine[n * phases : (n + 1) * phases] for n in range(6)]
    at_rim = dict(zip((-2, -1, 0, ny - 1, ny, ny + 1), rim_fine))

    beside = jnp.where(lane < 2 * ny, got[6], got[8])
    near = (lane < 4) | (lane >= nz - 4) & (lane < nz + 4) | (lane >= width - 4)
    rim = jnp.where(near, above[1], turn(below[0], 8))
    strips = exact_dot(jnp.concatenate([beside, rim], axis=1), strip_ref[width:])
    strips = strips + strips_ref[...]
    outer, side, inner, corner = (strips[:, n * width : (n + 1) * width] for n in range(4))
    near_labels = jnp.concatenate([got[9], got[7]], axis=1).astype(BF16)
    strip_labels = jnp.dot(near_labels, label_ref[...], preferred_element_type=F32)
    up = jnp.where(ends, corner, turn(side, 2))
    down = jnp.where((lane == width - 2) | (lane == width - 3), corner, turn(side, -2))
    side_base = side + rate * (outer + inner + up + down - side * (4.0 + total(side)))
    side1 = [
        side_base + jnp.where(strip_labels[:, n * width : (n + 1) * width] == phase_f, rate, 0.0)
        for n in range(2)
    ]

    def fine_row(y):
        if 0 < y < fy - 1:
            v = fine[y]
        else:
            (r0, a), (r1, b) = taps(y)
            v = a * at_rim[r0] + b * at_rim[r1]
        return jnp.where(ends, turn(inner, -2 * y), v) if 0 <= y < fy else v

    def pinned(n, y):
        if 0 <= y < fy:
            return pin[n, y]
        row = got[5, n : n + 1] if y < 0 else got[2, n : n + 1]
        return jnp.where(jnp.broadcast_to(row, shape) == phase_f, rate, 0.0)

    def halves(v):
        high = v.astype(BF16)
        return high, (v - high.astype(F32)).astype(BF16)

    def mixed(rows):
        flat = rows.reshape(-1, width)
        near = jnp.dot(
            jnp.concatenate(halves(flat), axis=1), beside_ref[...], preferred_element_type=F32
        )
        squares = jnp.dot(
            ones_ref[...], jnp.concatenate(halves(flat * flat), axis=0), preferred_element_type=F32
        )
        return near.reshape(rows.shape), squares.reshape(rows.shape)

    def sides(strip, block):
        at = range(8 * block, 8 * block + 8)
        return jnp.stack([jnp.where(ends, turn(strip, -2 * y), 0.0) for y in at])

    def first_row(y, prev, cur, nxt, beside_row):
        base = cur + rate * (prev + nxt + around(cur, beside_row) - cur * (4.0 + total(cur)))
        for n in range(2):
            p1[n, y + 1] = base + pinned(n, y)

    def first_step(block):
        rows = [fine_row(y) for y in range(8 * block - 1, 8 * block + 9)]
        cur = jnp.stack(rows[1:9])
        near, squares = mixed(cur)
        near = near + sides(side, block) + jnp.stack(rows[:8]) + jnp.stack(rows[2:])
        base = cur + rate * (near - cur * (4.0 + squares))
        for n in range(2):
            p1[n, 8 * block + 1 : 8 * block + 9] = base + pin[n, 8 * block : 8 * block + 8]

    out_rows = out_ref.reshape(fy // 8 * phases * 16, width)

    def second_step(block):
        y = 8 * block
        both = [p1[n, y + 1 : y + 9] for n in range(2)]
        for n in range(2):
            cur = both[n]
            near, squares = mixed(cur)
            near = near + sides(side1[n], block) + p1[n, y : y + 8] + p1[n, y + 2 : y + 10]
            near = near + 2.0 * both[1 - n]
            new = cur + rate * (near - cur * (6.0 + squares)) + pin[n, y : y + 8]
            for j in range(8):
                out_rows[pl.ds(block * phases * 16 + 8 * n + j, phases, stride=16)] = new[j]
        copy = pltpu.make_async_copy(
            out_ref.at[block], out_hbm.at[:, :, pl.ds(y, 8)], out_sem.at[block]
        )
        copy.start()
        return copy

    copies = []
    first_row(-1, fine_row(-2), fine_row(-1), fine_row(0), corner)
    first_row(fy, fine_row(fy - 1), fine_row(fy), fine_row(fy + 1), turn(corner, 2))
    first_step(0)
    for block in range(1, fy // 8):
        first_step(block)
        copies.append(second_step(block - 1))
    copies.append(second_step(fy // 8 - 1))
    for copy in copies:
        copy.wait()


def shards(gy, gz, coarse, labels, mobility):
    phases, planes, ny, nz = coarse.shape
    assert planes == 1 and labels.shape == (2, 2 * ny, 2 * nz) and ny <= nz // 2 and phases == 8
    width = 2 * nz
    vmem = pl.BlockSpec(memory_space=pltpu.VMEM)
    hbm = pl.BlockSpec(memory_space=pltpu.HBM)
    weights = [
        jnp.asarray(w, BF16)
        for w in (main_operator(nz), strip_operator(ny, nz), label_operator(ny, nz))
    ]
    sources = [pltpu.with_memory_space_constraint(v, pltpu.HBM) for v in (coarse, labels, mobility, *weights)]
    shared = [
        pltpu.VMEM((SLOTS, phases, width), F32),
        pltpu.VMEM((2 * ny, phases, width), F32),
        pltpu.VMEM((2, 2 * ny, phases, width), F32),
        pltpu.VMEM((phases, width), F32),
        pltpu.VMEM((phases, 4 * width), F32),
        pltpu.VMEM((2 * width, width), BF16),
        pltpu.VMEM((8 * phases, 16 * phases), BF16),
        *(pltpu.VMEM(v.shape, v.dtype) for v in weights),
    ]
    parts = pl.pallas_call(
        functools.partial(exchange, gy, gz),
        out_shape=shared,
        in_specs=[hbm] * len(sources),
        out_specs=[vmem] * len(shared),
        scratch_shapes=[
            pltpu.SMEM(mobility.shape, F32),
            pltpu.VMEM(labels.shape, jnp.int32),
            pltpu.VMEM(coarse.shape, F32),
            pltpu.VMEM((10, phases, width), F32),
            pltpu.SemaphoreType.DMA((len(PARTS),)),
            pltpu.SemaphoreType.DMA((len(PARTS),)),
            pltpu.SemaphoreType.DMA((len(sources),)),
        ],
        compiler_params=pltpu.CompilerParams(
            collective_id=0, has_side_effects=True, vmem_limit_bytes=8 * 2**20
        ),
        name="exchange",
    )(*sources)
    return pl.pallas_call(
        relax,
        out_shape=jax.ShapeDtypeStruct((phases, 2, 2 * ny, width), F32),
        in_specs=[vmem] * len(shared),
        out_specs=hbm,
        scratch_shapes=[
            pltpu.VMEM((2, 2 * ny + 2, phases, width), F32),
            pltpu.VMEM((2 * ny // 8, phases, 2, 8, width), F32),
            pltpu.SemaphoreType.DMA((2 * ny // 8,)),
        ],
        compiler_params=pltpu.CompilerParams(vmem_limit_bytes=8 * 2**20),
        name="relax",
    )(*parts)


def solution(mesh):
    in_specs = (P(None, None, "gy", "gz"), P(None, "gy", "gz"), P())
    out_specs = P(None, None, "gy", "gz")
    fn = functools.partial(shards, mesh.shape["gy"], mesh.shape["gz"])
    return jax.shard_map(fn, mesh=mesh, in_specs=in_specs, out_specs=out_specs, check_vma=False)
```

```python
import functools

import jax
import jax.numpy as jnp
import numpy as np
from jax import lax
from jax.experimental import pallas as pl
from jax.experimental.pallas import tpu as pltpu
from jax.sharding import PartitionSpec as P

STEP = 0.075
MESH = pl.DeviceIdType.MESH
F32 = jnp.float32
BF16 = jnp.bfloat16


def taps(cell):
    i = cell // 2
    return ((i, 0.75), (i + 1 if cell % 2 else i - 1, 0.25))


def col_lane(col, nz):
    return col % (2 * nz)


def main_operator(nz):
    width = 2 * nz
    w = np.zeros((width, width), np.float32)
    for z in range(width):
        for c, a in taps(z):
            w[col_lane(c, nz), z] += a
    return w


def strip_operator(ny, nz):
    width = 2 * nz

    def where(r, c):
        if r == -1:
            return 2 * width + col_lane(c, nz)
        if r == ny:
            return 2 * width + (col_lane(c, nz) + 8) % width
        assert 0 <= r < ny
        if c in (0, 1):
            return 2 * r + c
        if c in (nz - 2, nz - 1):
            return 2 * ny + 2 * r + c - (nz - 2)
        if c in (nz, nz + 1):
            return width + 2 * r + c - nz
        assert c in (-2, -1)
        return width + 2 * ny + 2 * r + c + 2

    w = np.zeros((3 * width, 4 * width), np.float32)

    def put(y, z, out):
        for r, a in taps(y):
            for c, b in taps(z):
                w[where(r, c), out] += a * b

    for y in range(2 * ny):
        left, right = 2 * y, (2 * y - 1) % width
        for block, (zl, zr) in enumerate(((-2, width + 1), (-1, width), (0, width - 1))):
            put(y, zl, block * width + left)
            put(y, zr, block * width + right)
    put(-1, -1, 3 * width)
    put(-1, width, 3 * width + width - 1)
    put(2 * ny, -1, 3 * width + width - 2)
    put(2 * ny, width, 3 * width + width - 3)
    return w


def label_operator(ny, nz):
    width = 2 * nz
    w = np.zeros((2 * width, 2 * width), np.float32)
    for x in range(2):
        for y in range(2 * ny):
            w[x * 2 * ny + y, x * width + 2 * y] = 1
            w[width + x * 2 * ny + y, x * width + (2 * y - 1) % width] = 1
    return w


PARTS = (
    ((-1, -1), (0, 2), (10, 12)),
    ((-1, 1), (0, 2), (12, 14)),
    ((1, -1), (3, 5), (14, 16)),
    ((1, 1), (3, 5), (16, 18)),
    ((0, -1), (6, 8), (6, 8)),
    ((0, 1), (8, 10), (8, 10)),
    ((-1, 0), (0, 3), (0, 3)),
    ((1, 0), (3, 6), (3, 6)),
)
SLOTS = 20


def wide(x):
    return jnp.concatenate([x, jnp.zeros_like(x)], axis=-1)


def exact_dot(x, w):
    high = x.astype(BF16).astype(F32)
    both = jnp.concatenate([high, x - high], axis=0).astype(BF16)
    product = jnp.dot(both, w, preferred_element_type=F32)
    return product[: x.shape[0]] + product[x.shape[0] :]


def exchange(gy, gz, *refs):
    sources, refs = refs[:6], refs[6:]
    got, fine_ref, pin_ref, rate_ref, strips_ref, beside_ref, ones_ref = refs[:7]
    main_ref, strip_ref, label_ref = refs[7:10]
    mobility_ref, labels_ref, coarse_ref, stage, send_sem, recv_sem, load_sem = refs[10:]
    me_y, me_z = lax.axis_index("gy"), lax.axis_index("gz")

    def other(dy, dz):
        return (lax.rem(me_y + dy + gy, gy), lax.rem(me_z + dz + gz, gz))

    barrier = pltpu.get_barrier_semaphore()
    for (dy, dz), _, _ in PARTS:
        pl.semaphore_signal(barrier, inc=1, device_id=other(dy, dz), device_id_type=MESH)
    targets = (coarse_ref, labels_ref, mobility_ref, main_ref, strip_ref, label_ref)
    loads = [
        pltpu.make_async_copy(source, target, load_sem.at[n])
        for n, (source, target) in enumerate(zip(sources, targets))
    ]
    for load in loads:
        load.start()

    phases, _, ny, nz = coarse_ref.shape
    width = 2 * nz
    lane = lax.broadcasted_iota(jnp.int32, (phases, width), 1)
    loads[0].wait()
    x = wide(jnp.swapaxes(coarse_ref[:, 0], 0, 1))
    rows = [x[r] for r in range(ny)]
    stage[0] = rows[0]
    stage[1] = rows[1]
    stage[3] = rows[ny - 2]
    stage[4] = rows[ny - 1]
    left = jnp.zeros((phases, width), F32)
    right = jnp.zeros((phases, width), F32)
    for r in range(ny):
        turned = rows[r] if r == 0 else pltpu.roll(rows[r], 2 * r, 1)
        left = jnp.where((lane >= 2 * r) & (lane < 2 * r + 2), turned, left)
        low = nz - 2 + 2 * r
        right = jnp.where((lane >= low) & (lane < low + 2), turned, right)
    right = pltpu.roll(right, (2 * ny - (nz - 2)) % width, 1)
    stage[6] = left
    stage[8] = right
    got[SLOTS - 2] = rows[0]
    got[SLOTS - 1] = rows[ny - 1]

    loads[1].wait()
    flat = labels_ref[...].reshape(-1, width).astype(F32).astype(BF16)

    def column(z):
        pick = (lane == z).astype(BF16)
        return lax.dot_general(
            pick, flat, (((1,), (1,)), ((), ())), preferred_element_type=F32
        )

    stage[2, 0:2] = labels_ref[:, 0].astype(F32)
    stage[5, 0:2] = labels_ref[:, 2 * ny - 1].astype(F32)
    stage[7] = column(0)
    stage[9] = column(width - 1)

    pl.semaphore_wait(barrier, len(PARTS))
    copies = []
    for n, ((dy, dz), (s0, s1), (d0, d1)) in enumerate(PARTS):
        copy = pltpu.make_async_remote_copy(
            src_ref=stage.at[s0:s1],
            dst_ref=got.at[d0:d1],
            send_sem=send_sem.at[n],
            recv_sem=recv_sem.at[n],
            device_id=other(dy, dz),
            device_id_type=MESH,
        )
        copy.start()
        copies.append(copy)

    phase_id = lax.broadcasted_iota(jnp.int32, (phases, width), 0)
    rate = jnp.zeros((phases, width), F32)
    loads[2].wait()
    for p in range(phases):
        rate = jnp.where(phase_id == p, STEP * mobility_ref[p], rate)
    rate_ref[...] = rate
    loads[3].wait()
    fine_z = exact_dot(x.reshape(-1, width), main_ref[...]).reshape(ny, phases, width)
    for y in range(1, 2 * ny - 1):
        (r0, a), (r1, b) = taps(y)
        fine_ref[y] = a * fine_z[r0] + b * fine_z[r1]
    for n in range(2):
        for y in range(2 * ny):
            label = jnp.broadcast_to(labels_ref[n, y : y + 1], rate.shape)
            pin_ref[n, y] = jnp.where(label == phase_id, rate, 0.0)
    row = lax.broadcasted_iota(jnp.int32, beside_ref.shape, 0) % width
    column_id = lax.broadcasted_iota(jnp.int32, beside_ref.shape, 1)
    beside_ref[...] = (jnp.abs(row - column_id) == 1).astype(F32).astype(BF16)
    row = lax.broadcasted_iota(jnp.int32, ones_ref.shape, 0)
    column_id = lax.broadcasted_iota(jnp.int32, ones_ref.shape, 1) % (8 * phases)
    ones_ref[...] = (row // phases == column_id // phases).astype(F32).astype(BF16)
    loads[4].wait()
    strips_ref[...] = exact_dot(left + right, strip_ref[:width])
    loads[5].wait()
    for copy in copies:
        copy.wait()


def relax(
    got, fine, pin, rate_ref, strips_ref, beside_ref, ones_ref, main_ref, strip_ref, label_ref, *rest
):
    out_hbm, p1, out_ref, out_sem = rest
    fy, phases, width = fine.shape
    ny, nz = fy // 2, width // 2
    shape = (phases, width)
    lane = lax.broadcasted_iota(jnp.int32, shape, 1)
    phase_id = lax.broadcasted_iota(jnp.int32, shape, 0)
    phase_f = phase_id.astype(F32)
    rate = rate_ref[...]
    first, last = lane == 0, lane == width - 1
    ends = first | last

    def turn(v, by):
        return pltpu.roll(v, by % width, 1) if by % width else v

    def total(v):
        return jnp.broadcast_to(jnp.sum(v * v, axis=0, keepdims=True), shape)

    def around(c, side):
        return jnp.where(first, side, turn(c, 1)) + jnp.where(last, side, turn(c, -1))

    halo_right = (lane >= nz) & (lane < nz + 2)
    halo_left = lane >= width - 2

    def edge(row, from_left, from_right, left_by=nz, right_by=nz):
        v = jnp.where(halo_right, turn(from_right, right_by), row)
        return jnp.where(halo_left, turn(from_left, left_by), v)

    below = [edge(got[n], got[12 + n], got[10 + n]) for n in range(2)]
    above = [edge(got[3 + n], got[16 + n], got[14 + n]) for n in range(2)]
    low = 2 * (ny - 1)
    top = edge(got[SLOTS - 2], got[8], got[6], width - 2 - 2 * ny, nz)
    bottom = edge(got[SLOTS - 1], got[8], got[6], width - 2 - 2 * ny - low, nz - low)
    rim_rows = jnp.concatenate([*above, top, bottom, *below], axis=0)
    rim_fine = exact_dot(rim_rows, main_ref[...])
    rim_fine = [rim_fine[n * phases : (n + 1) * phases] for n in range(6)]
    at_rim = dict(zip((-2, -1, 0, ny - 1, ny, ny + 1), rim_fine))

    beside = jnp.where(lane < 2 * ny, got[6], got[8])
    near = (lane < 4) | (lane >= nz - 4) & (lane < nz + 4) | (lane >= width - 4)
    rim = jnp.where(near, above[1], turn(below[0], 8))
    strips = exact_dot(jnp.concatenate([beside, rim], axis=1), strip_ref[width:])
    strips = strips + strips_ref[...]
    outer, side, inner, corner = (strips[:, n * width : (n + 1) * width] for n in range(4))
    near_labels = jnp.concatenate([got[9], got[7]], axis=1).astype(BF16)
    strip_labels = jnp.dot(near_labels, label_ref[...], preferred_element_type=F32)
    up = jnp.where(ends, corner, turn(side, 2))
    down = jnp.where((lane == width - 2) | (lane == width - 3), corner, turn(side, -2))
    side_base = side + rate * (outer + inner + up + down - side * (4.0 + total(side)))
    side1 = [
        side_base + jnp.where(strip_labels[:, n * width : (n + 1) * width] == phase_f, rate, 0.0)
        for n in range(2)
    ]

    def fine_row(y):
        if 0 < y < fy - 1:
            v = fine[y]
        else:
            (r0, a), (r1, b) = taps(y)
            v = a * at_rim[r0] + b * at_rim[r1]
        return jnp.where(ends, turn(inner, -2 * y), v) if 0 <= y < fy else v

    def pinned(n, y):
        if 0 <= y < fy:
            return pin[n, y]
        row = got[5, n : n + 1] if y < 0 else got[2, n : n + 1]
        return jnp.where(jnp.broadcast_to(row, shape) == phase_f, rate, 0.0)

    def halves(v):
        high = v.astype(BF16)
        return high, (v - high.astype(F32)).astype(BF16)

    def mixed(rows):
        flat = rows.reshape(-1, width)
        near = jnp.dot(
            jnp.concatenate(halves(flat), axis=1), beside_ref[...], preferred_element_type=F32
        )
        tall = 8 * phases
        squares = [
            jnp.dot(
                ones_ref[...],
                jnp.concatenate(halves(part * part), axis=0),
                preferred_element_type=F32,
            )
            for part in (flat[at : at + tall] for at in range(0, flat.shape[0], tall))
        ]
        squares = jnp.concatenate(squares, axis=0)
        return near.reshape(rows.shape), squares.reshape(rows.shape)

    def sides(strip, at):
        return jnp.stack([jnp.where(ends, turn(strip, -2 * y), 0.0) for y in at])

    def first_row(y, prev, cur, nxt, beside_row):
        base = cur + rate * (prev + nxt + around(cur, beside_row) - cur * (4.0 + total(cur)))
        for n in range(2):
            p1[n, y + 1] = base + pinned(n, y)

    def first_step():
        rows = [fine_row(y) for y in range(-1, fy + 1)]
        cur = jnp.stack(rows[1:-1])
        near, squares = mixed(cur)
        near = near + sides(side, range(fy)) + jnp.stack(rows[:-2]) + jnp.stack(rows[2:])
        base = cur + rate * (near - cur * (4.0 + squares))
        for n in range(2):
            p1[n, 1 : fy + 1] = base + pin[n]

    chunks, _, _, tall, _ = out_ref.shape
    out_rows = out_ref.reshape(chunks * phases * 2 * tall, width)

    def second_step(chunk):
        y = tall * chunk
        both = [p1[n, y + 1 : y + tall + 1] for n in range(2)]
        for n in range(2):
            cur = both[n]
            near, squares = mixed(cur)
            near = near + sides(side1[n], range(y, y + tall))
            near = near + p1[n, y : y + tall] + p1[n, y + 2 : y + tall + 2]
            near = near + 2.0 * both[1 - n]
            new = cur + rate * (near - cur * (6.0 + squares)) + pin[n, y : y + tall]
            for j in range(tall):
                at = (chunk * phases * 2 + n) * tall + j
                out_rows[pl.ds(at, phases, stride=2 * tall)] = new[j]
        copy = pltpu.make_async_copy(
            out_ref.at[chunk], out_hbm.at[:, :, pl.ds(y, tall)], out_sem.at[chunk]
        )
        copy.start()
        return copy

    first_row(-1, fine_row(-2), fine_row(-1), fine_row(0), corner)
    first_row(fy, fine_row(fy - 1), fine_row(fy), fine_row(fy + 1), turn(corner, 2))
    first_step()
    copies = [second_step(chunk) for chunk in range(chunks)]
    for copy in copies:
        copy.wait()


def shards(gy, gz, coarse, labels, mobility):
    phases, planes, ny, nz = coarse.shape
    assert planes == 1 and labels.shape == (2, 2 * ny, 2 * nz) and ny <= nz // 2 and phases == 8
    width = 2 * nz
    vmem = pl.BlockSpec(memory_space=pltpu.VMEM)
    hbm = pl.BlockSpec(memory_space=pltpu.HBM)
    weights = [
        jnp.asarray(w, BF16)
        for w in (main_operator(nz), strip_operator(ny, nz), label_operator(ny, nz))
    ]
    sources = [pltpu.with_memory_space_constraint(v, pltpu.HBM) for v in (coarse, labels, mobility, *weights)]
    shared = [
        pltpu.VMEM((SLOTS, phases, width), F32),
        pltpu.VMEM((2 * ny, phases, width), F32),
        pltpu.VMEM((2, 2 * ny, phases, width), F32),
        pltpu.VMEM((phases, width), F32),
        pltpu.VMEM((phases, 4 * width), F32),
        pltpu.VMEM((2 * width, width), BF16),
        pltpu.VMEM((8 * phases, 16 * phases), BF16),
        *(pltpu.VMEM(v.shape, v.dtype) for v in weights),
    ]
    parts = pl.pallas_call(
        functools.partial(exchange, gy, gz),
        out_shape=shared,
        in_specs=[hbm] * len(sources),
        out_specs=[vmem] * len(shared),
        scratch_shapes=[
            pltpu.SMEM(mobility.shape, F32),
            pltpu.VMEM(labels.shape, jnp.int32),
            pltpu.VMEM(coarse.shape, F32),
            pltpu.VMEM((10, phases, width), F32),
            pltpu.SemaphoreType.DMA((len(PARTS),)),
            pltpu.SemaphoreType.DMA((len(PARTS),)),
            pltpu.SemaphoreType.DMA((len(sources),)),
        ],
        compiler_params=pltpu.CompilerParams(
            collective_id=0, has_side_effects=True, vmem_limit_bytes=8 * 2**20
        ),
        name="exchange",
    )(*sources)
    return pl.pallas_call(
        relax,
        out_shape=jax.ShapeDtypeStruct((phases, 2, 2 * ny, width), F32),
        in_specs=[vmem] * len(shared),
        out_specs=hbm,
        scratch_shapes=[
            pltpu.VMEM((2, 2 * ny + 2, phases, width), F32),
            pltpu.VMEM((2, phases, 2, ny, width), F32),
            pltpu.SemaphoreType.DMA((2,)),
        ],
        compiler_params=pltpu.CompilerParams(vmem_limit_bytes=8 * 2**20),
        name="relax",
    )(*parts)


def solution(mesh):
    in_specs = (P(None, None, "gy", "gz"), P(None, "gy", "gz"), P())
    out_specs = P(None, None, "gy", "gz")
    fn = functools.partial(shards, mesh.shape["gy"], mesh.shape["gz"])
    return jax.shard_map(fn, mesh=mesh, in_specs=in_specs, out_specs=out_specs, check_vma=False)
```

```python
import functools

import jax
import jax.numpy as jnp
import numpy as np
from jax import lax
from jax.experimental import pallas as pl
from jax.experimental.pallas import tpu as pltpu
from jax.sharding import PartitionSpec as P

STEP = 0.075
MESH = pl.DeviceIdType.MESH
F32 = jnp.float32
BF16 = jnp.bfloat16


def taps(cell):
    i = cell // 2
    return ((i, 0.75), (i + 1 if cell % 2 else i - 1, 0.25))


def col_lane(col, nz):
    return col % (2 * nz)


def main_operator(nz):
    width = 2 * nz
    w = np.zeros((width, width), np.float32)
    for z in range(width):
        for c, a in taps(z):
            w[col_lane(c, nz), z] += a
    return w


def strip_operator(ny, nz):
    width = 2 * nz

    def where(r, c):
        if r == -1:
            return 3 * width + col_lane(c, nz)
        if r == ny:
            return 3 * width + (col_lane(c, nz) + 8) % width
        assert 0 <= r < ny
        if c in (0, 1):
            return 2 * r + c
        if c in (nz - 2, nz - 1):
            return 2 * ny + 2 * r + c - (nz - 2)
        if c in (2, nz - 3):
            return width + (2 * r + c) % width
        if c in (nz, nz + 1):
            return 2 * width + 2 * r + c - nz
        assert c in (-2, -1)
        return 2 * width + 2 * ny + 2 * r + c + 2

    w = np.zeros((4 * width, 8 * width), np.float32)

    def put(y, z, out):
        for r, a in taps(y):
            for c, b in taps(z):
                w[where(r, c), out] += a * b

    for y in range(2 * ny):
        left, right = 2 * y, (2 * y - 1) % width
        for block, k in ((0, -2), (1, -1), (2, 0), (4, 1), (5, 2), (6, 3), (7, 4)):
            put(y, k, block * width + left)
            put(y, width - 1 - k, block * width + right)
    put(-1, -1, 3 * width)
    put(-1, width, 3 * width + width - 1)
    put(2 * ny, -1, 3 * width + width - 2)
    put(2 * ny, width, 3 * width + width - 3)
    return w


def label_operator(ny, nz):
    width = 2 * nz
    w = np.zeros((2 * width, 2 * width), np.float32)
    for x in range(2):
        for y in range(2 * ny):
            w[x * 2 * ny + y, x * width + 2 * y] = 1
            w[width + x * 2 * ny + y, x * width + (2 * y - 1) % width] = 1
    return w


PARTS = (
    ((-1, -1), (0, 2), (10, 12)),
    ((-1, 1), (0, 2), (12, 14)),
    ((1, -1), (3, 5), (14, 16)),
    ((1, 1), (3, 5), (16, 18)),
    ((0, -1), (6, 8), (6, 8)),
    ((0, 1), (8, 10), (8, 10)),
    ((-1, 0), (0, 3), (0, 3)),
    ((1, 0), (3, 6), (3, 6)),
)
SLOTS = 20


def wide(x):
    return jnp.concatenate([x, jnp.zeros_like(x)], axis=-1)


def exact_dot(x, w):
    high = x.astype(BF16).astype(F32)
    both = jnp.concatenate([high, x - high], axis=0).astype(BF16)
    product = jnp.dot(both, w, preferred_element_type=F32)
    return product[: x.shape[0]] + product[x.shape[0] :]


def halves(v):
    high = v.astype(BF16)
    return high, (v - high.astype(F32)).astype(BF16)


def mixed(rows, beside, ones):
    _, phases, width = rows.shape
    flat = rows.reshape(-1, width)
    near = jnp.dot(jnp.concatenate(halves(flat), axis=1), beside, preferred_element_type=F32)
    tall = 8 * phases
    squares = [
        jnp.dot(
            ones, jnp.concatenate(halves(part * part), axis=0), preferred_element_type=F32
        )
        for part in (flat[at : at + tall] for at in range(0, flat.shape[0], tall))
    ]
    return near.reshape(rows.shape), jnp.concatenate(squares, axis=0).reshape(rows.shape)


def above_below(rows):
    return jnp.concatenate([rows[:1], rows[:-1]]) + jnp.concatenate([rows[1:], rows[-1:]])


def exchange(gy, gz, *refs):
    sources, refs = refs[:6], refs[6:]
    got, fine_ref, inner_ref, pin_ref, rate_ref, strips_ref, side_pin_ref = refs[:7]
    main_ref, strip_ref, label_ref = refs[7:10]
    mobility_ref, labels_ref, coarse_ref, stage, send_sem, recv_sem, load_sem = refs[10:]
    me_y, me_z = lax.axis_index("gy"), lax.axis_index("gz")

    def other(dy, dz):
        return (lax.rem(me_y + dy + gy, gy), lax.rem(me_z + dz + gz, gz))

    barrier = pltpu.get_barrier_semaphore()
    for (dy, dz), _, _ in PARTS:
        pl.semaphore_signal(barrier, inc=1, device_id=other(dy, dz), device_id_type=MESH)
    targets = (coarse_ref, labels_ref, mobility_ref, main_ref, strip_ref, label_ref)
    loads = [
        pltpu.make_async_copy(source, target, load_sem.at[n])
        for n, (source, target) in enumerate(zip(sources, targets))
    ]
    for load in loads:
        load.start()

    phases, _, ny, nz = coarse_ref.shape
    width = 2 * nz
    lane = lax.broadcasted_iota(jnp.int32, (phases, width), 1)
    loads[0].wait()
    x = wide(jnp.swapaxes(coarse_ref[:, 0], 0, 1))
    rows = [x[r] for r in range(ny)]
    stage[0] = rows[0]
    stage[1] = rows[1]
    stage[3] = rows[ny - 2]
    stage[4] = rows[ny - 1]
    left = jnp.zeros((phases, width), F32)
    right = jnp.zeros((phases, width), F32)
    for r in range(ny):
        turned = rows[r] if r == 0 else pltpu.roll(rows[r], 2 * r, 1)
        left = jnp.where((lane >= 2 * r) & (lane < 2 * r + 2), turned, left)
        low = nz - 2 + 2 * r
        right = jnp.where((lane >= low) & (lane < low + 2), turned, right)
    right = pltpu.roll(right, (2 * ny - (nz - 2)) % width, 1)
    stage[6] = left
    stage[8] = right
    got[SLOTS - 2] = rows[0]
    got[SLOTS - 1] = rows[ny - 1]

    loads[1].wait()
    flat = labels_ref[...].reshape(-1, width).astype(F32).astype(BF16)

    def column(z):
        pick = (lane == z).astype(BF16)
        return lax.dot_general(
            pick, flat, (((1,), (1,)), ((), ())), preferred_element_type=F32
        )

    stage[2, 0:2] = labels_ref[:, 0].astype(F32)
    stage[5, 0:2] = labels_ref[:, 2 * ny - 1].astype(F32)
    stage[7] = column(0)
    stage[9] = column(width - 1)

    pl.semaphore_wait(barrier, len(PARTS))
    copies = []
    for n, ((dy, dz), (s0, s1), (d0, d1)) in enumerate(PARTS):
        copy = pltpu.make_async_remote_copy(
            src_ref=stage.at[s0:s1],
            dst_ref=got.at[d0:d1],
            send_sem=send_sem.at[n],
            recv_sem=recv_sem.at[n],
            device_id=other(dy, dz),
            device_id_type=MESH,
        )
        copy.start()
        copies.append(copy)

    phase_id = lax.broadcasted_iota(jnp.int32, (phases, width), 0)
    rate = jnp.zeros((phases, width), F32)
    loads[2].wait()
    for p in range(phases):
        rate = jnp.where(phase_id == p, STEP * mobility_ref[p], rate)
    rate_ref[...] = rate
    loads[3].wait()
    fine_z = exact_dot(x.reshape(-1, width), main_ref[...]).reshape(ny, phases, width)
    fine_ref[0], fine_ref[2 * ny - 1] = fine_z[0], fine_z[ny - 1]
    for y in range(1, 2 * ny - 1):
        (r0, a), (r1, b) = taps(y)
        fine_ref[y] = a * fine_z[r0] + b * fine_z[r1]
    for n in range(2):
        for y in range(2 * ny):
            label = jnp.broadcast_to(labels_ref[n, y : y + 1], rate.shape)
            pin_ref[n, y] = jnp.where(label == phase_id, rate, 0.0)

    loads[4].wait()
    third = jnp.zeros((phases, width), F32)
    for r in range(ny):
        hit = (lane == (2 * r + 2) % width) | (lane == (2 * r + nz - 3) % width)
        third = jnp.where(hit, pltpu.roll(rows[r], 2 * r, 1) if r else rows[r], third)
    strips_ref[...] = exact_dot(
        jnp.concatenate([left + right, third], axis=1), strip_ref[: 2 * width]
    )
    loads[5].wait()
    edge_lane = jnp.where(phase_id < 4, phase_id, width - 1 - (phase_id - 4))
    edge_labels = lax.dot_general(
        (lane == edge_lane).astype(BF16), flat, (((1,), (1,)), ((), ())), preferred_element_type=F32
    ).astype(BF16)
    from_left = jnp.dot(edge_labels, label_ref[:width], preferred_element_type=F32)
    from_right = jnp.dot(edge_labels, label_ref[width:], preferred_element_type=F32)
    for k in range(4):
        label = from_left[k : k + 1] + from_right[4 + k : 5 + k]
        for n in range(2):
            one = jnp.broadcast_to(label[:, n * width : (n + 1) * width], rate.shape)
            side_pin_ref[k, n] = jnp.where(one == phase_id.astype(F32), rate, 0.0)

    row = lax.broadcasted_iota(jnp.int32, (2 * width, width), 0) % width
    column_id = lax.broadcasted_iota(jnp.int32, (2 * width, width), 1)
    beside = (jnp.abs(row - column_id) == 1).astype(F32).astype(BF16)
    row = lax.broadcasted_iota(jnp.int32, (8 * phases, 16 * phases), 0)
    column_id = lax.broadcasted_iota(jnp.int32, (8 * phases, 16 * phases), 1) % (8 * phases)
    ones = (row // phases == column_id // phases).astype(F32).astype(BF16)
    cur = fine_ref[...]
    near, squares = mixed(cur, beside, ones)
    base = cur + rate * (near + above_below(cur) - cur * (4.0 + squares))
    both = [base + pin_ref[n] for n in range(2)]
    for n in range(2):
        cur = both[n]
        near, squares = mixed(cur, beside, ones)
        near = near + above_below(cur) + 2.0 * both[1 - n]
        inner_ref[n] = cur + rate * (near - cur * (6.0 + squares)) + pin_ref[n]
    for copy in copies:
        copy.wait()


def relax(got, fine, inner, pin, rate_ref, strips_ref, side_pin, main_ref, strip_ref, label_ref, *rest):
    out_hbm, out_ref, out_sem = rest
    fy, phases, width = fine.shape
    ny, nz = fy // 2, width // 2
    shape = (phases, width)
    lane = lax.broadcasted_iota(jnp.int32, shape, 1)
    phase_f = lax.broadcasted_iota(jnp.int32, shape, 0).astype(F32)
    rate = rate_ref[...]
    first, last = lane == 0, lane == width - 1
    ends = first | last

    def turn(v, by):
        return pltpu.roll(v, by % width, 1) if by % width else v

    def total(v):
        return jnp.broadcast_to(jnp.sum(v * v, axis=0, keepdims=True), shape)

    def around(c, side):
        return jnp.where(first, side, turn(c, 1)) + jnp.where(last, side, turn(c, -1))

    halo_right = (lane >= nz) & (lane < nz + 2)
    halo_left = lane >= width - 2

    def edge(row, from_left, from_right, left_by=nz, right_by=nz):
        v = jnp.where(halo_right, turn(from_right, right_by), row)
        return jnp.where(halo_left, turn(from_left, left_by), v)

    below = [edge(got[n], got[12 + n], got[10 + n]) for n in range(2)]
    above = [edge(got[3 + n], got[16 + n], got[14 + n]) for n in range(2)]
    low = 2 * (ny - 1)
    top = edge(got[SLOTS - 2], got[8], got[6], width - 2 - 2 * ny, nz)
    bottom = edge(got[SLOTS - 1], got[8], got[6], width - 2 - 2 * ny - low, nz - low)
    rim_rows = jnp.concatenate([*above, top, bottom, *below], axis=0)
    rim_fine = exact_dot(rim_rows, main_ref[...])
    rim_fine = [rim_fine[n * phases : (n + 1) * phases] for n in range(6)]
    at_rim = dict(zip((-2, -1, 0, ny - 1, ny, ny + 1), rim_fine))

    beside = jnp.where(lane < 2 * ny, got[6], got[8])
    near = (lane < 4) | (lane >= nz - 4) & (lane < nz + 4) | (lane >= width - 4)
    rim = jnp.where(near, above[1], turn(below[0], 8))
    strips = exact_dot(jnp.concatenate([beside, rim], axis=1), strip_ref[2 * width :])
    strips = strips + strips_ref[...]
    blocks = [strips[:, n * width : (n + 1) * width] for n in range(8)]
    corner = blocks.pop(3)
    fine_at = dict(zip(range(-2, 5), blocks))
    near_labels = jnp.concatenate([got[9], got[7]], axis=1).astype(BF16)
    strip_labels = jnp.dot(near_labels, label_ref[...], preferred_element_type=F32)

    def side_pinned(k, n):
        if k >= 0:
            return side_pin[k, n]
        return jnp.where(strip_labels[:, n * width : (n + 1) * width] == phase_f, rate, 0.0)

    step1 = {}
    for k in range(-1, 4):
        c = fine_at[k]
        up, down = turn(c, 2), turn(c, -2)
        if k < 0:
            up = jnp.where(ends, corner, up)
            down = jnp.where((lane == width - 2) | (lane == width - 3), corner, down)
        near = fine_at[k - 1] + fine_at[k + 1] + up + down
        base = c + rate * (near - c * (4.0 + total(c)))
        step1[k] = [base + side_pinned(k, n) for n in range(2)]
    side, side1 = fine_at[-1], step1[-1]
    step2 = {}
    for k in range(3):
        step2[k] = []
        for n in range(2):
            c = step1[k][n]
            near = step1[k - 1][n] + step1[k + 1][n] + turn(c, 2) + turn(c, -2)
            near = near + 2.0 * step1[k][1 - n]
            new = c + rate * (near - c * (6.0 + total(c))) + side_pin[k, n]
            if k:
                new = jnp.where(lane % 2 == k % 2, turn(new, k), turn(new, -k))
            step2[k].append(new)

    def fine_row(y):
        if 0 < y < fy - 1:
            v = fine[y]
        else:
            (r0, a), (r1, b) = taps(y)
            v = a * at_rim[r0] + b * at_rim[r1]
        return jnp.where(ends, turn(fine_at[0], -2 * y), v) if 0 <= y < fy else v

    def pinned(n, y):
        if 0 <= y < fy:
            return pin[n, y]
        row = got[5, n : n + 1] if y < 0 else got[2, n : n + 1]
        return jnp.where(jnp.broadcast_to(row, shape) == phase_f, rate, 0.0)

    def first_row(y):
        prev, cur, nxt = (fine_row(v) for v in (y - 1, y, y + 1))
        if y < 0:
            beside_row = corner
        elif y == fy:
            beside_row = turn(corner, 2)
        else:
            beside_row = turn(side, -2 * y)
        base = cur + rate * (prev + nxt + around(cur, beside_row) - cur * (4.0 + total(cur)))
        return [base + pinned(n, y) for n in range(2)]

    rim1 = {y: first_row(y) for y in (*range(-1, 4), *range(fy - 4, fy + 1))}
    at_column = [(lane == k) | (lane == width - 1 - k) for k in range(3)]

    def second_row(n, y):
        if 3 <= y < fy - 3:
            new = inner[n, y]
            for k in range(3):
                new = jnp.where(at_column[k], turn(step2[k][n], -2 * y), new)
            return new
        c = rim1[y][n]
        near = rim1[y - 1][n] + rim1[y + 1][n] + around(c, turn(side1[n], -2 * y))
        near = near + 2.0 * rim1[y][1 - n]
        return c + rate * (near - c * (6.0 + total(c))) + pinned(n, y)

    chunks, _, _, tall, _ = out_ref.shape
    out_rows = out_ref.reshape(chunks * phases * 2 * tall, width)
    copies = []
    for chunk in range(chunks):
        for n in range(2):
            for j in range(tall):
                at = (chunk * phases * 2 + n) * tall + j
                row = second_row(n, chunk * tall + j)
                out_rows[pl.ds(at, phases, stride=2 * tall)] = row
        copy = pltpu.make_async_copy(
            out_ref.at[chunk], out_hbm.at[:, :, pl.ds(chunk * tall, tall)], out_sem.at[chunk]
        )
        copy.start()
        copies.append(copy)
    for copy in copies:
        copy.wait()


def shards(gy, gz, coarse, labels, mobility):
    phases, planes, ny, nz = coarse.shape
    assert planes == 1 and labels.shape == (2, 2 * ny, 2 * nz) and ny <= nz // 2 and phases == 8
    width = 2 * nz
    vmem = pl.BlockSpec(memory_space=pltpu.VMEM)
    hbm = pl.BlockSpec(memory_space=pltpu.HBM)
    weights = [
        jnp.asarray(w, BF16)
        for w in (main_operator(nz), strip_operator(ny, nz), label_operator(ny, nz))
    ]
    sources = [pltpu.with_memory_space_constraint(v, pltpu.HBM) for v in (coarse, labels, mobility, *weights)]
    shared = [
        pltpu.VMEM((SLOTS, phases, width), F32),
        pltpu.VMEM((2 * ny, phases, width), F32),
        pltpu.VMEM((2, 2 * ny, phases, width), F32),
        pltpu.VMEM((2, 2 * ny, phases, width), F32),
        pltpu.VMEM((phases, width), F32),
        pltpu.VMEM((phases, 8 * width), F32),
        pltpu.VMEM((4, 2, phases, width), F32),
        *(pltpu.VMEM(v.shape, v.dtype) for v in weights),
    ]
    parts = pl.pallas_call(
        functools.partial(exchange, gy, gz),
        out_shape=shared,
        in_specs=[hbm] * len(sources),
        out_specs=[vmem] * len(shared),
        scratch_shapes=[
            pltpu.SMEM(mobility.shape, F32),
            pltpu.VMEM(labels.shape, jnp.int32),
            pltpu.VMEM(coarse.shape, F32),
            pltpu.VMEM((10, phases, width), F32),
            pltpu.SemaphoreType.DMA((len(PARTS),)),
            pltpu.SemaphoreType.DMA((len(PARTS),)),
            pltpu.SemaphoreType.DMA((len(sources),)),
        ],
        compiler_params=pltpu.CompilerParams(
            collective_id=0, has_side_effects=True, vmem_limit_bytes=12 * 2**20
        ),
        name="exchange",
    )(*sources)
    return pl.pallas_call(
        relax,
        out_shape=jax.ShapeDtypeStruct((phases, 2, 2 * ny, width), F32),
        in_specs=[vmem] * len(shared),
        out_specs=hbm,
        scratch_shapes=[
            pltpu.VMEM((2, phases, 2, ny, width), F32),
            pltpu.SemaphoreType.DMA((2,)),
        ],
        compiler_params=pltpu.CompilerParams(vmem_limit_bytes=12 * 2**20),
        name="relax",
    )(*parts)


def solution(mesh):
    in_specs = (P(None, None, "gy", "gz"), P(None, "gy", "gz"), P())
    out_specs = P(None, None, "gy", "gz")
    fn = functools.partial(shards, mesh.shape["gy"], mesh.shape["gz"])
    return jax.shard_map(fn, mesh=mesh, in_specs=in_specs, out_specs=out_specs, check_vma=False)
```

```python
import functools

import jax
import jax.numpy as jnp
import numpy as np
from jax import lax
from jax.experimental import pallas as pl
from jax.experimental.pallas import tpu as pltpu
from jax.sharding import PartitionSpec as P

STEP = 0.075
MESH = pl.DeviceIdType.MESH
F32 = jnp.float32
BF16 = jnp.bfloat16


def taps(cell):
    i = cell // 2
    return ((i, 0.75), (i + 1 if cell % 2 else i - 1, 0.25))


def col_lane(col, nz):
    return col % (2 * nz)


def main_operator(nz):
    width = 2 * nz
    w = np.zeros((width, width), np.float32)
    for z in range(width):
        for c, a in taps(z):
            w[col_lane(c, nz), z] += a
    return w


def strip_operator(ny, nz):
    width = 2 * nz

    def where(r, c):
        if r == -1:
            return 3 * width + col_lane(c, nz)
        if r == ny:
            return 3 * width + (col_lane(c, nz) + 8) % width
        assert 0 <= r < ny
        if c in (0, 1):
            return 2 * r + c
        if c in (nz - 2, nz - 1):
            return 2 * ny + 2 * r + c - (nz - 2)
        if c in (2, nz - 3):
            return width + (2 * r + c) % width
        if c in (nz, nz + 1):
            return 2 * width + 2 * r + c - nz
        assert c in (-2, -1)
        return 2 * width + 2 * ny + 2 * r + c + 2

    w = np.zeros((4 * width, 8 * width), np.float32)

    def put(y, z, out):
        for r, a in taps(y):
            for c, b in taps(z):
                w[where(r, c), out] += a * b

    for y in range(2 * ny):
        left, right = 2 * y, (2 * y - 1) % width
        for block, k in ((0, -2), (1, -1), (2, 0), (4, 1), (5, 2), (6, 3), (7, 4)):
            put(y, k, block * width + left)
            put(y, width - 1 - k, block * width + right)
    put(-1, -1, 3 * width)
    put(-1, width, 3 * width + width - 1)
    put(2 * ny, -1, 3 * width + width - 2)
    put(2 * ny, width, 3 * width + width - 3)
    return w


def label_operator(ny, nz):
    width = 2 * nz
    w = np.zeros((2 * width, 2 * width), np.float32)
    for x in range(2):
        for y in range(2 * ny):
            w[x * 2 * ny + y, x * width + 2 * y] = 1
            w[width + x * 2 * ny + y, x * width + (2 * y - 1) % width] = 1
    return w


PARTS = (
    ((-1, -1), (0, 2), (10, 12)),
    ((-1, 1), (0, 2), (12, 14)),
    ((1, -1), (3, 5), (14, 16)),
    ((1, 1), (3, 5), (16, 18)),
    ((0, -1), (6, 8), (6, 8)),
    ((0, 1), (8, 10), (8, 10)),
    ((-1, 0), (0, 3), (0, 3)),
    ((1, 0), (3, 6), (3, 6)),
)
SLOTS = 20


def wide(x):
    return jnp.concatenate([x, jnp.zeros_like(x)], axis=-1)


def exact_dot(x, w):
    high = x.astype(BF16).astype(F32)
    both = jnp.concatenate([high, x - high], axis=0).astype(BF16)
    product = jnp.dot(both, w, preferred_element_type=F32)
    return product[: x.shape[0]] + product[x.shape[0] :]


def halves(v):
    high = v.astype(BF16)
    return high, (v - high.astype(F32)).astype(BF16)


def mixed(rows, beside, ones):
    _, phases, width = rows.shape
    flat = rows.reshape(-1, width)
    near = jnp.dot(jnp.concatenate(halves(flat), axis=1), beside, preferred_element_type=F32)
    tall = 8 * phases
    squares = [
        jnp.dot(
            ones, jnp.concatenate(halves(part * part), axis=0), preferred_element_type=F32
        )
        for part in (flat[at : at + tall] for at in range(0, flat.shape[0], tall))
    ]
    return near.reshape(rows.shape), jnp.concatenate(squares, axis=0).reshape(rows.shape)


def above_below(rows):
    return jnp.concatenate([rows[:1], rows[:-1]]) + jnp.concatenate([rows[1:], rows[-1:]])


def exchange(gy, gz, *refs):
    sources, refs = refs[:6], refs[6:]
    got, fine_ref, inner_ref, pin_ref, rate_ref, strips_ref, side_pin_ref = refs[:7]
    main_ref, strip_ref, label_ref = refs[7:10]
    mobility_ref, labels_ref, coarse_ref, stage, send_sem, recv_sem, load_sem = refs[10:]
    me_y, me_z = lax.axis_index("gy"), lax.axis_index("gz")

    def other(dy, dz):
        return (lax.rem(me_y + dy + gy, gy), lax.rem(me_z + dz + gz, gz))

    barrier = pltpu.get_barrier_semaphore()
    for (dy, dz), _, _ in PARTS:
        pl.semaphore_signal(barrier, inc=1, device_id=other(dy, dz), device_id_type=MESH)
    targets = (coarse_ref, labels_ref, mobility_ref, main_ref, strip_ref, label_ref)
    loads = [
        pltpu.make_async_copy(source, target, load_sem.at[n])
        for n, (source, target) in enumerate(zip(sources, targets))
    ]
    for load in loads:
        load.start()

    phases, _, ny, nz = coarse_ref.shape
    width = 2 * nz
    lane = lax.broadcasted_iota(jnp.int32, (phases, width), 1)
    loads[0].wait()
    x = wide(jnp.swapaxes(coarse_ref[:, 0], 0, 1))
    rows = [x[r] for r in range(ny)]
    stage[0] = rows[0]
    stage[1] = rows[1]
    stage[3] = rows[ny - 2]
    stage[4] = rows[ny - 1]
    left = jnp.zeros((phases, width), F32)
    right = jnp.zeros((phases, width), F32)
    for r in range(ny):
        turned = rows[r] if r == 0 else pltpu.roll(rows[r], 2 * r, 1)
        left = jnp.where((lane >= 2 * r) & (lane < 2 * r + 2), turned, left)
        low = nz - 2 + 2 * r
        right = jnp.where((lane >= low) & (lane < low + 2), turned, right)
    right = pltpu.roll(right, (2 * ny - (nz - 2)) % width, 1)
    stage[6] = left
    stage[8] = right
    got[SLOTS - 2] = rows[0]
    got[SLOTS - 1] = rows[ny - 1]

    loads[1].wait()
    flat = labels_ref[...].reshape(-1, width).astype(F32).astype(BF16)

    def column(z):
        pick = (lane == z).astype(BF16)
        return lax.dot_general(
            pick, flat, (((1,), (1,)), ((), ())), preferred_element_type=F32
        )

    stage[2, 0:2] = labels_ref[:, 0].astype(F32)
    stage[5, 0:2] = labels_ref[:, 2 * ny - 1].astype(F32)
    stage[7] = column(0)
    stage[9] = column(width - 1)

    pl.semaphore_wait(barrier, len(PARTS))
    copies = []
    for n, ((dy, dz), (s0, s1), (d0, d1)) in enumerate(PARTS):
        copy = pltpu.make_async_remote_copy(
            src_ref=stage.at[s0:s1],
            dst_ref=got.at[d0:d1],
            send_sem=send_sem.at[n],
            recv_sem=recv_sem.at[n],
            device_id=other(dy, dz),
            device_id_type=MESH,
        )
        copy.start()
        copies.append(copy)

    phase_id = lax.broadcasted_iota(jnp.int32, (phases, width), 0)
    rate = jnp.zeros((phases, width), F32)
    loads[2].wait()
    for p in range(phases):
        rate = jnp.where(phase_id == p, STEP * mobility_ref[p], rate)
    rate_ref[...] = rate
    loads[3].wait()
    fine_z = exact_dot(x.reshape(-1, width), main_ref[...]).reshape(ny, phases, width)
    fine_ref[0], fine_ref[2 * ny - 1] = fine_z[0], fine_z[ny - 1]
    for y in range(1, 2 * ny - 1):
        (r0, a), (r1, b) = taps(y)
        fine_ref[y] = a * fine_z[r0] + b * fine_z[r1]
    for n in range(2):
        for y in range(2 * ny):
            label = jnp.broadcast_to(labels_ref[n, y : y + 1], rate.shape)
            pin_ref[n, y] = jnp.where(label == phase_id, rate, 0.0)

    loads[4].wait()
    third = jnp.zeros((phases, width), F32)
    for r in range(ny):
        hit = (lane == (2 * r + 2) % width) | (lane == (2 * r + nz - 3) % width)
        third = jnp.where(hit, pltpu.roll(rows[r], 2 * r, 1) if r else rows[r], third)
    strips_ref[...] = exact_dot(
        jnp.concatenate([left + right, third], axis=1), strip_ref[: 2 * width]
    )
    loads[5].wait()
    edge_lane = jnp.where(phase_id < 4, phase_id, width - 1 - (phase_id - 4))
    edge_labels = lax.dot_general(
        (lane == edge_lane).astype(BF16), flat, (((1,), (1,)), ((), ())), preferred_element_type=F32
    ).astype(BF16)
    from_left = jnp.dot(edge_labels, label_ref[:width], preferred_element_type=F32)
    from_right = jnp.dot(edge_labels, label_ref[width:], preferred_element_type=F32)
    for k in range(4):
        label = from_left[k : k + 1] + from_right[4 + k : 5 + k]
        for n in range(2):
            one = jnp.broadcast_to(label[:, n * width : (n + 1) * width], rate.shape)
            side_pin_ref[k, n] = jnp.where(one == phase_id.astype(F32), rate, 0.0)

    row = lax.broadcasted_iota(jnp.int32, (2 * width, width), 0) % width
    column_id = lax.broadcasted_iota(jnp.int32, (2 * width, width), 1)
    beside = (jnp.abs(row - column_id) == 1).astype(F32).astype(BF16)
    row = lax.broadcasted_iota(jnp.int32, (8 * phases, 16 * phases), 0)
    column_id = lax.broadcasted_iota(jnp.int32, (8 * phases, 16 * phases), 1) % (8 * phases)
    ones = (row // phases == column_id // phases).astype(F32).astype(BF16)
    cur = fine_ref[...]
    near, squares = mixed(cur, beside, ones)
    base = cur + rate * (near + above_below(cur) - cur * (4.0 + squares))
    both = [base + pin_ref[n] for n in range(2)]
    for n in range(2):
        cur = both[n]
        near, squares = mixed(cur, beside, ones)
        near = near + above_below(cur) + 2.0 * both[1 - n]
        inner_ref[n] = cur + rate * (near - cur * (6.0 + squares)) + pin_ref[n]
    for copy in copies:
        copy.wait()


def relax(got, fine, inner, pin, rate_ref, strips_ref, side_pin, main_ref, strip_ref, label_ref, *rest):
    out_hbm, out_ref, out_sem = rest
    fy, phases, width = fine.shape
    ny, nz = fy // 2, width // 2
    shape = (phases, width)
    lane = lax.broadcasted_iota(jnp.int32, shape, 1)
    phase_f = lax.broadcasted_iota(jnp.int32, shape, 0).astype(F32)
    rate = rate_ref[...]
    first, last = lane == 0, lane == width - 1
    ends = first | last

    def turn(v, by):
        return pltpu.roll(v, by % width, 1) if by % width else v

    def total(v):
        return jnp.broadcast_to(jnp.sum(v * v, axis=0, keepdims=True), shape)

    def around(c, side):
        return jnp.where(first, side, turn(c, 1)) + jnp.where(last, side, turn(c, -1))

    halo_right = (lane >= nz) & (lane < nz + 2)
    halo_left = lane >= width - 2

    def edge(row, from_left, from_right, left_by=nz, right_by=nz):
        v = jnp.where(halo_right, turn(from_right, right_by), row)
        return jnp.where(halo_left, turn(from_left, left_by), v)

    below = [edge(got[n], got[12 + n], got[10 + n]) for n in range(2)]
    above = [edge(got[3 + n], got[16 + n], got[14 + n]) for n in range(2)]
    low = 2 * (ny - 1)
    top = edge(got[SLOTS - 2], got[8], got[6], width - 2 - 2 * ny, nz)
    bottom = edge(got[SLOTS - 1], got[8], got[6], width - 2 - 2 * ny - low, nz - low)
    rim_rows = jnp.concatenate([*above, top, bottom, *below], axis=0)
    rim_fine = exact_dot(rim_rows, main_ref[...])
    rim_fine = [rim_fine[n * phases : (n + 1) * phases] for n in range(6)]
    at_rim = dict(zip((-2, -1, 0, ny - 1, ny, ny + 1), rim_fine))

    beside = jnp.where(lane < 2 * ny, got[6], got[8])
    near = (lane < 4) | (lane >= nz - 4) & (lane < nz + 4) | (lane >= width - 4)
    rim = jnp.where(near, above[1], turn(below[0], 8))
    strips = exact_dot(jnp.concatenate([beside, rim], axis=1), strip_ref[2 * width :])
    strips = strips + strips_ref[...]
    pieces = [strips[:, n * width : (n + 1) * width] for n in range(8)]
    corner = pieces.pop(3)
    fine_at = dict(zip(range(-2, 5), pieces))
    near_labels = jnp.concatenate([got[9], got[7]], axis=1).astype(BF16)
    strip_labels = jnp.dot(near_labels, label_ref[...], preferred_element_type=F32)

    def side_pinned(k, n):
        if k >= 0:
            return side_pin[k, n]
        return jnp.where(strip_labels[:, n * width : (n + 1) * width] == phase_f, rate, 0.0)

    step1 = {}
    for k in range(-1, 4):
        c = fine_at[k]
        up, down = turn(c, 2), turn(c, -2)
        if k < 0:
            up = jnp.where(ends, corner, up)
            down = jnp.where((lane == width - 2) | (lane == width - 3), corner, down)
        near = fine_at[k - 1] + fine_at[k + 1] + up + down
        base = c + rate * (near - c * (4.0 + total(c)))
        step1[k] = [base + side_pinned(k, n) for n in range(2)]
    side, side1 = fine_at[-1], step1[-1]
    step2 = {}
    for k in range(3):
        step2[k] = []
        for n in range(2):
            c = step1[k][n]
            near = step1[k - 1][n] + step1[k + 1][n] + turn(c, 2) + turn(c, -2)
            near = near + 2.0 * step1[k][1 - n]
            new = c + rate * (near - c * (6.0 + total(c))) + side_pin[k, n]
            if k:
                new = jnp.where(lane % 2 == k % 2, turn(new, k), turn(new, -k))
            step2[k].append(new)

    def fine_row(y):
        if 0 < y < fy - 1:
            v = fine[y]
        else:
            (r0, a), (r1, b) = taps(y)
            v = a * at_rim[r0] + b * at_rim[r1]
        return jnp.where(ends, turn(fine_at[0], -2 * y), v) if 0 <= y < fy else v

    def pinned(n, y):
        if 0 <= y < fy:
            return pin[n, y]
        row = got[5, n : n + 1] if y < 0 else got[2, n : n + 1]
        return jnp.where(jnp.broadcast_to(row, shape) == phase_f, rate, 0.0)

    def first_row(y):
        prev, cur, nxt = (fine_row(v) for v in (y - 1, y, y + 1))
        if y < 0:
            beside_row = corner
        elif y == fy:
            beside_row = turn(corner, 2)
        else:
            beside_row = turn(side, -2 * y)
        base = cur + rate * (prev + nxt + around(cur, beside_row) - cur * (4.0 + total(cur)))
        return [base + pinned(n, y) for n in range(2)]

    rim1 = {y: first_row(y) for y in (*range(-1, 4), *range(fy - 4, fy + 1))}
    at_column = [(lane == k) | (lane == width - 1 - k) for k in range(3)]

    def merged(row, columns, by):
        for k in range(3):
            row = jnp.where(at_column[k], turn(columns[k], by), row)
        return row

    def second_row(n, y):
        if 3 <= y < fy - 3:
            return merged(inner[n, y], [step2[k][n] for k in range(3)], -2 * y)
        c = rim1[y][n]
        near = rim1[y - 1][n] + rim1[y + 1][n] + around(c, turn(side1[n], -2 * y))
        near = near + 2.0 * rim1[y][1 - n]
        return c + rate * (near - c * (6.0 + total(c))) + pinned(n, y)

    blocks, _, _, tall, _ = out_ref.shape
    out_rows = out_ref.reshape(blocks, phases * 2 * tall, width)

    def send(block):
        return pltpu.make_async_copy(
            out_ref.at[block],
            out_hbm.at[:, :, pl.ds(pl.multiple_of(block * tall, tall), tall)],
            out_sem.at[block],
        )

    def store(block, n, j, row):
        out_rows[block, pl.ds(n * tall + j, phases, stride=2 * tall)] = row

    for block in (0, blocks - 1):
        for n in range(2):
            for j in range(tall):
                store(block, n, j, second_row(n, block * tall + j))
        send(block).start()

    def body(block, columns):
        columns = [[turn(v, -2 * tall) for v in plane] for plane in columns]
        for n in range(2):
            for j in range(tall):
                store(block, n, j, merged(inner[n, block * tall + j], columns[n], -2 * j))
        send(block).start()
        return columns

    lax.fori_loop(1, blocks - 1, body, [[step2[k][n] for k in range(3)] for n in range(2)])
    for block in range(blocks):
        send(block).wait()


def shards(gy, gz, coarse, labels, mobility):
    phases, planes, ny, nz = coarse.shape
    assert planes == 1 and labels.shape == (2, 2 * ny, 2 * nz) and ny <= nz // 2 and phases == 8
    width = 2 * nz
    vmem = pl.BlockSpec(memory_space=pltpu.VMEM)
    hbm = pl.BlockSpec(memory_space=pltpu.HBM)
    weights = [
        jnp.asarray(w, BF16)
        for w in (main_operator(nz), strip_operator(ny, nz), label_operator(ny, nz))
    ]
    sources = [pltpu.with_memory_space_constraint(v, pltpu.HBM) for v in (coarse, labels, mobility, *weights)]
    shared = [
        pltpu.VMEM((SLOTS, phases, width), F32),
        pltpu.VMEM((2 * ny, phases, width), F32),
        pltpu.VMEM((2, 2 * ny, phases, width), F32),
        pltpu.VMEM((2, 2 * ny, phases, width), F32),
        pltpu.VMEM((phases, width), F32),
        pltpu.VMEM((phases, 8 * width), F32),
        pltpu.VMEM((4, 2, phases, width), F32),
        *(pltpu.VMEM(v.shape, v.dtype) for v in weights),
    ]
    parts = pl.pallas_call(
        functools.partial(exchange, gy, gz),
        out_shape=shared,
        in_specs=[hbm] * len(sources),
        out_specs=[vmem] * len(shared),
        scratch_shapes=[
            pltpu.SMEM(mobility.shape, F32),
            pltpu.VMEM(labels.shape, jnp.int32),
            pltpu.VMEM(coarse.shape, F32),
            pltpu.VMEM((10, phases, width), F32),
            pltpu.SemaphoreType.DMA((len(PARTS),)),
            pltpu.SemaphoreType.DMA((len(PARTS),)),
            pltpu.SemaphoreType.DMA((len(sources),)),
        ],
        compiler_params=pltpu.CompilerParams(
            collective_id=0, has_side_effects=True, vmem_limit_bytes=12 * 2**20
        ),
        name="exchange",
    )(*sources)
    return pl.pallas_call(
        relax,
        out_shape=jax.ShapeDtypeStruct((phases, 2, 2 * ny, width), F32),
        in_specs=[vmem] * len(shared),
        out_specs=hbm,
        scratch_shapes=[
            pltpu.VMEM((2 * ny // 8, phases, 2, 8, width), F32),
            pltpu.SemaphoreType.DMA((2 * ny // 8,)),
        ],
        compiler_params=pltpu.CompilerParams(vmem_limit_bytes=12 * 2**20),
        name="relax",
    )(*parts)


def solution(mesh):
    in_specs = (P(None, None, "gy", "gz"), P(None, "gy", "gz"), P())
    out_specs = P(None, None, "gy", "gz")
    fn = functools.partial(shards, mesh.shape["gy"], mesh.shape["gz"])
    return jax.shard_map(fn, mesh=mesh, in_specs=in_specs, out_specs=out_specs, check_vma=False)
```

```python
import functools

import jax
import jax.numpy as jnp
import numpy as np
from jax import lax
from jax.experimental import pallas as pl
from jax.experimental.pallas import tpu as pltpu
from jax.sharding import PartitionSpec as P

STEP = 0.075
MESH = pl.DeviceIdType.MESH
F32 = jnp.float32
BF16 = jnp.bfloat16


def taps(cell):
    i = cell // 2
    return ((i, 0.75), (i + 1 if cell % 2 else i - 1, 0.25))


def col_lane(col, nz):
    return col % (2 * nz)


def main_operator(nz):
    width = 2 * nz
    w = np.zeros((width, width), np.float32)
    for z in range(width):
        for c, a in taps(z):
            w[col_lane(c, nz), z] += a
    return w


def strip_operator(ny, nz):
    width = 2 * nz

    def where(r, c):
        if r == -1:
            return 3 * width + col_lane(c, nz)
        if r == ny:
            return 3 * width + (col_lane(c, nz) + 8) % width
        assert 0 <= r < ny
        if c in (0, 1):
            return 2 * r + c
        if c in (nz - 2, nz - 1):
            return 2 * ny + 2 * r + c - (nz - 2)
        if c in (2, nz - 3):
            return width + (2 * r + c) % width
        if c in (nz, nz + 1):
            return 2 * width + 2 * r + c - nz
        assert c in (-2, -1)
        return 2 * width + 2 * ny + 2 * r + c + 2

    w = np.zeros((4 * width, 8 * width), np.float32)

    def put(y, z, out):
        for r, a in taps(y):
            for c, b in taps(z):
                w[where(r, c), out] += a * b

    for y in range(2 * ny):
        left, right = 2 * y, (2 * y - 1) % width
        for block, k in ((0, -2), (1, -1), (2, 0), (4, 1), (5, 2), (6, 3), (7, 4)):
            put(y, k, block * width + left)
            put(y, width - 1 - k, block * width + right)
    put(-1, -1, 3 * width)
    put(-1, width, 3 * width + width - 1)
    put(2 * ny, -1, 3 * width + width - 2)
    put(2 * ny, width, 3 * width + width - 3)
    return w


def label_operator(ny, nz):
    width = 2 * nz
    w = np.zeros((2 * width, 2 * width), np.float32)
    for x in range(2):
        for y in range(2 * ny):
            w[x * 2 * ny + y, x * width + 2 * y] = 1
            w[width + x * 2 * ny + y, x * width + (2 * y - 1) % width] = 1
    return w


PARTS = (
    ((-1, -1), (0, 2), (10, 12)),
    ((-1, 1), (0, 2), (12, 14)),
    ((1, -1), (3, 5), (14, 16)),
    ((1, 1), (3, 5), (16, 18)),
    ((0, -1), (6, 8), (6, 8)),
    ((0, 1), (8, 10), (8, 10)),
    ((-1, 0), (0, 3), (0, 3)),
    ((1, 0), (3, 6), (3, 6)),
)
SLOTS = 20


def wide(x):
    return jnp.concatenate([x, jnp.zeros_like(x)], axis=-1)


def exact_dot(x, w):
    high = x.astype(BF16).astype(F32)
    both = jnp.concatenate([high, x - high], axis=0).astype(BF16)
    product = jnp.dot(both, w, preferred_element_type=F32)
    return product[: x.shape[0]] + product[x.shape[0] :]


def halves(v):
    high = v.astype(BF16)
    return high, (v - high.astype(F32)).astype(BF16)


def mixed(rows, beside, ones):
    _, phases, width = rows.shape
    flat = rows.reshape(-1, width)
    near = jnp.dot(jnp.concatenate(halves(flat), axis=1), beside, preferred_element_type=F32)
    tall = 8 * phases
    squares = [
        jnp.dot(
            ones, jnp.concatenate(halves(part * part), axis=0), preferred_element_type=F32
        )
        for part in (flat[at : at + tall] for at in range(0, flat.shape[0], tall))
    ]
    return near.reshape(rows.shape), jnp.concatenate(squares, axis=0).reshape(rows.shape)


def above_below(rows):
    return jnp.concatenate([rows[:1], rows[:-1]]) + jnp.concatenate([rows[1:], rows[-1:]])


def exchange(gy, gz, *refs):
    sources, refs = refs[:6], refs[6:]
    got, fine_ref, inner_ref, pin_ref, rate_ref, strips_ref, side_pin_ref = refs[:7]
    main_ref, strip_ref, label_ref = refs[7:10]
    mobility_ref, labels_ref, coarse_ref, stage, send_sem, recv_sem, load_sem = refs[10:]
    me_y, me_z = lax.axis_index("gy"), lax.axis_index("gz")

    def other(dy, dz):
        return (lax.rem(me_y + dy + gy, gy), lax.rem(me_z + dz + gz, gz))

    barrier = pltpu.get_barrier_semaphore()
    for (dy, dz), _, _ in PARTS:
        pl.semaphore_signal(barrier, inc=1, device_id=other(dy, dz), device_id_type=MESH)
    targets = (coarse_ref, labels_ref, mobility_ref, main_ref, strip_ref, label_ref)
    loads = [
        pltpu.make_async_copy(source, target, load_sem.at[n])
        for n, (source, target) in enumerate(zip(sources, targets))
    ]
    for load in loads:
        load.start()

    phases, _, ny, nz = coarse_ref.shape
    width = 2 * nz
    lane = lax.broadcasted_iota(jnp.int32, (phases, width), 1)
    loads[0].wait()
    x = wide(jnp.swapaxes(coarse_ref[:, 0], 0, 1))
    rows = [x[r] for r in range(ny)]
    stage[0] = rows[0]
    stage[1] = rows[1]
    stage[3] = rows[ny - 2]
    stage[4] = rows[ny - 1]
    left = jnp.zeros((phases, width), F32)
    right = jnp.zeros((phases, width), F32)
    for r in range(ny):
        turned = rows[r] if r == 0 else pltpu.roll(rows[r], 2 * r, 1)
        left = jnp.where((lane >= 2 * r) & (lane < 2 * r + 2), turned, left)
        low = nz - 2 + 2 * r
        right = jnp.where((lane >= low) & (lane < low + 2), turned, right)
    right = pltpu.roll(right, (2 * ny - (nz - 2)) % width, 1)
    stage[6] = left
    stage[8] = right
    got[SLOTS - 2] = rows[0]
    got[SLOTS - 1] = rows[ny - 1]

    loads[1].wait()
    flat = labels_ref[...].reshape(-1, width).astype(F32).astype(BF16)

    def column(z):
        pick = (lane == z).astype(BF16)
        return lax.dot_general(
            pick, flat, (((1,), (1,)), ((), ())), preferred_element_type=F32
        )

    stage[2, 0:2] = labels_ref[:, 0].astype(F32)
    stage[5, 0:2] = labels_ref[:, 2 * ny - 1].astype(F32)
    stage[7] = column(0)
    stage[9] = column(width - 1)

    pl.semaphore_wait(barrier, len(PARTS))
    copies = []
    for n, ((dy, dz), (s0, s1), (d0, d1)) in enumerate(PARTS):
        copy = pltpu.make_async_remote_copy(
            src_ref=stage.at[s0:s1],
            dst_ref=got.at[d0:d1],
            send_sem=send_sem.at[n],
            recv_sem=recv_sem.at[n],
            device_id=other(dy, dz),
            device_id_type=MESH,
        )
        copy.start()
        copies.append(copy)

    phase_id = lax.broadcasted_iota(jnp.int32, (phases, width), 0)
    rate = jnp.zeros((phases, width), F32)
    loads[2].wait()
    for p in range(phases):
        rate = jnp.where(phase_id == p, STEP * mobility_ref[p], rate)
    rate_ref[...] = rate
    loads[3].wait()
    fine_z = exact_dot(x.reshape(-1, width), main_ref[...]).reshape(ny, phases, width)
    fine_ref[0], fine_ref[2 * ny - 1] = fine_z[0], fine_z[ny - 1]
    for y in range(1, 2 * ny - 1):
        (r0, a), (r1, b) = taps(y)
        fine_ref[y] = a * fine_z[r0] + b * fine_z[r1]
    for n in range(2):
        for y in range(2 * ny):
            label = jnp.broadcast_to(labels_ref[n, y : y + 1], rate.shape)
            pin_ref[n, y] = jnp.where(label == phase_id, rate, 0.0)

    loads[4].wait()
    third = jnp.zeros((phases, width), F32)
    for r in range(ny):
        hit = (lane == (2 * r + 2) % width) | (lane == (2 * r + nz - 3) % width)
        third = jnp.where(hit, pltpu.roll(rows[r], 2 * r, 1) if r else rows[r], third)
    strips_ref[...] = exact_dot(
        jnp.concatenate([left + right, third], axis=1), strip_ref[: 2 * width]
    )
    loads[5].wait()
    edge_lane = jnp.where(phase_id < 4, phase_id, width - 1 - (phase_id - 4))
    edge_labels = lax.dot_general(
        (lane == edge_lane).astype(BF16), flat, (((1,), (1,)), ((), ())), preferred_element_type=F32
    ).astype(BF16)
    from_left = jnp.dot(edge_labels, label_ref[:width], preferred_element_type=F32)
    from_right = jnp.dot(edge_labels, label_ref[width:], preferred_element_type=F32)
    for k in range(4):
        label = from_left[k : k + 1] + from_right[4 + k : 5 + k]
        for n in range(2):
            one = jnp.broadcast_to(label[:, n * width : (n + 1) * width], rate.shape)
            side_pin_ref[k, n] = jnp.where(one == phase_id.astype(F32), rate, 0.0)

    row = lax.broadcasted_iota(jnp.int32, (2 * width, width), 0) % width
    column_id = lax.broadcasted_iota(jnp.int32, (2 * width, width), 1)
    beside = (jnp.abs(row - column_id) == 1).astype(F32).astype(BF16)
    row = lax.broadcasted_iota(jnp.int32, (8 * phases, 16 * phases), 0)
    column_id = lax.broadcasted_iota(jnp.int32, (8 * phases, 16 * phases), 1) % (8 * phases)
    ones = (row // phases == column_id // phases).astype(F32).astype(BF16)
    cur = fine_ref[...]
    near, squares = mixed(cur, beside, ones)
    base = cur + rate * (near + above_below(cur) - cur * (4.0 + squares))
    both = [base + pin_ref[n] for n in range(2)]
    for n in range(2):
        cur = both[n]
        near, squares = mixed(cur, beside, ones)
        near = near + above_below(cur) + 2.0 * both[1 - n]
        inner_ref[n] = cur + rate * (near - cur * (6.0 + squares)) + pin_ref[n]
    for copy in copies:
        copy.wait()


def relax(got, fine, inner, pin, rate_ref, strips_ref, side_pin, main_ref, strip_ref, label_ref, *rest):
    (out_ref,) = rest
    fy, phases, width = fine.shape
    ny, nz = fy // 2, width // 2
    shape = (phases, width)
    lane = lax.broadcasted_iota(jnp.int32, shape, 1)
    phase_f = lax.broadcasted_iota(jnp.int32, shape, 0).astype(F32)
    rate = rate_ref[...]
    first, last = lane == 0, lane == width - 1
    ends = first | last

    def turn(v, by):
        return pltpu.roll(v, by % width, 1) if by % width else v

    def total(v):
        return jnp.broadcast_to(jnp.sum(v * v, axis=0, keepdims=True), shape)

    def around(c, side):
        return jnp.where(first, side, turn(c, 1)) + jnp.where(last, side, turn(c, -1))

    halo_right = (lane >= nz) & (lane < nz + 2)
    halo_left = lane >= width - 2

    def edge(row, from_left, from_right, left_by=nz, right_by=nz):
        v = jnp.where(halo_right, turn(from_right, right_by), row)
        return jnp.where(halo_left, turn(from_left, left_by), v)

    below = [edge(got[n], got[12 + n], got[10 + n]) for n in range(2)]
    above = [edge(got[3 + n], got[16 + n], got[14 + n]) for n in range(2)]
    low = 2 * (ny - 1)
    top = edge(got[SLOTS - 2], got[8], got[6], width - 2 - 2 * ny, nz)
    bottom = edge(got[SLOTS - 1], got[8], got[6], width - 2 - 2 * ny - low, nz - low)
    rim_rows = jnp.concatenate([*above, top, bottom, *below], axis=0)
    rim_fine = exact_dot(rim_rows, main_ref[...])
    rim_fine = [rim_fine[n * phases : (n + 1) * phases] for n in range(6)]
    at_rim = dict(zip((-2, -1, 0, ny - 1, ny, ny + 1), rim_fine))

    beside = jnp.where(lane < 2 * ny, got[6], got[8])
    near = (lane < 4) | (lane >= nz - 4) & (lane < nz + 4) | (lane >= width - 4)
    rim = jnp.where(near, above[1], turn(below[0], 8))
    strips = exact_dot(jnp.concatenate([beside, rim], axis=1), strip_ref[2 * width :])
    strips = strips + strips_ref[...]
    blocks = [strips[:, n * width : (n + 1) * width] for n in range(8)]
    corner = blocks.pop(3)
    fine_at = dict(zip(range(-2, 5), blocks))
    near_labels = jnp.concatenate([got[9], got[7]], axis=1).astype(BF16)
    strip_labels = jnp.dot(near_labels, label_ref[...], preferred_element_type=F32)

    def side_pinned(k, n):
        if k >= 0:
            return side_pin[k, n]
        return jnp.where(strip_labels[:, n * width : (n + 1) * width] == phase_f, rate, 0.0)

    step1 = {}
    for k in range(-1, 4):
        c = fine_at[k]
        up, down = turn(c, 2), turn(c, -2)
        if k < 0:
            up = jnp.where(ends, corner, up)
            down = jnp.where((lane == width - 2) | (lane == width - 3), corner, down)
        near = fine_at[k - 1] + fine_at[k + 1] + up + down
        base = c + rate * (near - c * (4.0 + total(c)))
        step1[k] = [base + side_pinned(k, n) for n in range(2)]
    side, side1 = fine_at[-1], step1[-1]
    step2 = {}
    for k in range(3):
        step2[k] = []
        for n in range(2):
            c = step1[k][n]
            near = step1[k - 1][n] + step1[k + 1][n] + turn(c, 2) + turn(c, -2)
            near = near + 2.0 * step1[k][1 - n]
            new = c + rate * (near - c * (6.0 + total(c))) + side_pin[k, n]
            if k:
                new = jnp.where(lane % 2 == k % 2, turn(new, k), turn(new, -k))
            step2[k].append(new)

    def fine_row(y):
        if 0 < y < fy - 1:
            v = fine[y]
        else:
            (r0, a), (r1, b) = taps(y)
            v = a * at_rim[r0] + b * at_rim[r1]
        return jnp.where(ends, turn(fine_at[0], -2 * y), v) if 0 <= y < fy else v

    def pinned(n, y):
        if 0 <= y < fy:
            return pin[n, y]
        row = got[5, n : n + 1] if y < 0 else got[2, n : n + 1]
        return jnp.where(jnp.broadcast_to(row, shape) == phase_f, rate, 0.0)

    def first_row(y):
        prev, cur, nxt = (fine_row(v) for v in (y - 1, y, y + 1))
        if y < 0:
            beside_row = corner
        elif y == fy:
            beside_row = turn(corner, 2)
        else:
            beside_row = turn(side, -2 * y)
        base = cur + rate * (prev + nxt + around(cur, beside_row) - cur * (4.0 + total(cur)))
        return [base + pinned(n, y) for n in range(2)]

    rim1 = {y: first_row(y) for y in (*range(-1, 4), *range(fy - 4, fy + 1))}
    at_column = [(lane == k) | (lane == width - 1 - k) for k in range(3)]

    def second_row(n, y):
        if 3 <= y < fy - 3:
            new = inner[n, y]
            for k in range(3):
                new = jnp.where(at_column[k], turn(step2[k][n], -2 * y), new)
            return new
        c = rim1[y][n]
        near = rim1[y - 1][n] + rim1[y + 1][n] + around(c, turn(side1[n], -2 * y))
        near = near + 2.0 * rim1[y][1 - n]
        return c + rate * (near - c * (6.0 + total(c))) + pinned(n, y)

    out_rows = out_ref.reshape(phases * 2 * fy, width)
    for n in range(2):
        for y in range(fy):
            out_rows[pl.ds(n * fy + y, phases, stride=2 * fy)] = second_row(n, y)


def whole(gy, gz, *refs):
    sources, out_ref, shared, rest = refs[:6], refs[6], refs[7:17], refs[17:]
    exchange(gy, gz, *sources, *shared, *rest)
    relax(*shared, out_ref)


def shards(gy, gz, coarse, labels, mobility):
    phases, planes, ny, nz = coarse.shape
    assert planes == 1 and labels.shape == (2, 2 * ny, 2 * nz) and ny <= nz // 2 and phases == 8
    width = 2 * nz
    vmem = pl.BlockSpec(memory_space=pltpu.VMEM)
    hbm = pl.BlockSpec(memory_space=pltpu.HBM)
    weights = [
        jnp.asarray(w, BF16)
        for w in (main_operator(nz), strip_operator(ny, nz), label_operator(ny, nz))
    ]
    sources = [pltpu.with_memory_space_constraint(v, pltpu.HBM) for v in (coarse, labels, mobility, *weights)]
    shared = [
        pltpu.VMEM((SLOTS, phases, width), F32),
        pltpu.VMEM((2 * ny, phases, width), F32),
        pltpu.VMEM((2, 2 * ny, phases, width), F32),
        pltpu.VMEM((2, 2 * ny, phases, width), F32),
        pltpu.VMEM((phases, width), F32),
        pltpu.VMEM((phases, 8 * width), F32),
        pltpu.VMEM((4, 2, phases, width), F32),
        *(pltpu.VMEM(v.shape, v.dtype) for v in weights),
    ]
    return pl.pallas_call(
        functools.partial(whole, gy, gz),
        out_shape=pltpu.VMEM((phases, 2, 2 * ny, width), F32),
        in_specs=[hbm] * len(sources),
        out_specs=vmem,
        scratch_shapes=[
            *shared,
            pltpu.SMEM(mobility.shape, F32),
            pltpu.VMEM(labels.shape, jnp.int32),
            pltpu.VMEM(coarse.shape, F32),
            pltpu.VMEM((10, phases, width), F32),
            pltpu.SemaphoreType.DMA((len(PARTS),)),
            pltpu.SemaphoreType.DMA((len(PARTS),)),
            pltpu.SemaphoreType.DMA((len(sources),)),
        ],
        compiler_params=pltpu.CompilerParams(
            collective_id=0, has_side_effects=True, vmem_limit_bytes=16 * 2**20
        ),
        name="relax",
    )(*sources)


def solution(mesh):
    in_specs = (P(None, None, "gy", "gz"), P(None, "gy", "gz"), P())
    out_specs = P(None, None, "gy", "gz")
    fn = functools.partial(shards, mesh.shape["gy"], mesh.shape["gz"])
    return jax.shard_map(fn, mesh=mesh, in_specs=in_specs, out_specs=out_specs, check_vma=False)
```

```python
import functools

import jax
import jax.numpy as jnp
import numpy as np
from jax import lax
from jax.experimental import pallas as pl
from jax.experimental.pallas import tpu as pltpu
from jax.sharding import PartitionSpec as P

STEP = 0.075
MESH = pl.DeviceIdType.MESH
F32 = jnp.float32
BF16 = jnp.bfloat16


def taps(cell):
    i = cell // 2
    return ((i, 0.75), (i + 1 if cell % 2 else i - 1, 0.25))


def col_lane(col, nz):
    return col % (2 * nz)


def main_operator(nz):
    width = 2 * nz
    w = np.zeros((width, width), np.float32)
    for z in range(width):
        for c, a in taps(z):
            w[col_lane(c, nz), z] += a
    return w


def strip_operator(ny, nz):
    width = 2 * nz

    def where(r, c):
        if r == -1:
            return 3 * width + col_lane(c, nz)
        if r == ny:
            return 3 * width + (col_lane(c, nz) + 8) % width
        assert 0 <= r < ny
        if c in (0, 1):
            return 2 * r + c
        if c in (nz - 2, nz - 1):
            return 2 * ny + 2 * r + c - (nz - 2)
        if c in (2, nz - 3):
            return width + (2 * r + c) % width
        if c in (nz, nz + 1):
            return 2 * width + 2 * r + c - nz
        assert c in (-2, -1)
        return 2 * width + 2 * ny + 2 * r + c + 2

    w = np.zeros((4 * width, 8 * width), np.float32)

    def put(y, z, out):
        for r, a in taps(y):
            for c, b in taps(z):
                w[where(r, c), out] += a * b

    for y in range(2 * ny):
        left, right = 2 * y, (2 * y - 1) % width
        for block, k in ((0, -2), (1, -1), (2, 0), (4, 1), (5, 2), (6, 3), (7, 4)):
            put(y, k, block * width + left)
            put(y, width - 1 - k, block * width + right)
    put(-1, -1, 3 * width)
    put(-1, width, 3 * width + width - 1)
    put(2 * ny, -1, 3 * width + width - 2)
    put(2 * ny, width, 3 * width + width - 3)
    return w


def label_operator(ny, nz):
    width = 2 * nz
    w = np.zeros((2 * width, 2 * width), np.float32)
    for x in range(2):
        for y in range(2 * ny):
            w[x * 2 * ny + y, x * width + 2 * y] = 1
            w[width + x * 2 * ny + y, x * width + (2 * y - 1) % width] = 1
    return w


PARTS = (
    ((-1, -1), (0, 2), (10, 12)),
    ((-1, 1), (0, 2), (12, 14)),
    ((1, -1), (3, 5), (14, 16)),
    ((1, 1), (3, 5), (16, 18)),
    ((0, -1), (6, 8), (6, 8)),
    ((0, 1), (8, 10), (8, 10)),
    ((-1, 0), (0, 3), (0, 3)),
    ((1, 0), (3, 6), (3, 6)),
)
SLOTS = 20


def wide(x):
    return jnp.concatenate([x, jnp.zeros_like(x)], axis=-1)


def exact_dot(x, w):
    high = x.astype(BF16).astype(F32)
    both = jnp.concatenate([high, x - high], axis=0).astype(BF16)
    product = jnp.dot(both, w, preferred_element_type=F32)
    return product[: x.shape[0]] + product[x.shape[0] :]


def halves(v):
    high = v.astype(BF16)
    return high, (v - high.astype(F32)).astype(BF16)


def mixed(rows, beside, ones):
    _, phases, width = rows.shape
    flat = rows.reshape(-1, width)
    near = jnp.dot(jnp.concatenate(halves(flat), axis=1), beside, preferred_element_type=F32)
    tall = 8 * phases
    squares = [
        jnp.dot(
            ones, jnp.concatenate(halves(part * part), axis=0), preferred_element_type=F32
        )
        for part in (flat[at : at + tall] for at in range(0, flat.shape[0], tall))
    ]
    return near.reshape(rows.shape), jnp.concatenate(squares, axis=0).reshape(rows.shape)


def above_below(rows):
    return jnp.concatenate([rows[:1], rows[:-1]]) + jnp.concatenate([rows[1:], rows[-1:]])


def exchange(gy, gz, *refs):
    sources, refs = refs[:6], refs[6:]
    got, fine_ref, inner_ref, pin_ref, rate_ref, strips_ref, side_pin_ref = refs[:7]
    main_ref, strip_ref, label_ref = refs[7:10]
    mobility_ref, labels_ref, coarse_ref, stage, send_sem, recv_sem, load_sem = refs[10:]
    me_y, me_z = lax.axis_index("gy"), lax.axis_index("gz")

    def other(dy, dz):
        return (lax.rem(me_y + dy + gy, gy), lax.rem(me_z + dz + gz, gz))

    barrier = pltpu.get_barrier_semaphore()
    for (dy, dz), _, _ in PARTS:
        pl.semaphore_signal(barrier, inc=1, device_id=other(dy, dz), device_id_type=MESH)
    targets = (coarse_ref, labels_ref, mobility_ref, main_ref, strip_ref, label_ref)
    loads = [
        pltpu.make_async_copy(source, target, load_sem.at[n])
        for n, (source, target) in enumerate(zip(sources, targets))
    ]
    for load in loads:
        load.start()

    phases, _, ny, nz = coarse_ref.shape
    width = 2 * nz
    lane = lax.broadcasted_iota(jnp.int32, (phases, width), 1)
    loads[0].wait()
    x = wide(jnp.swapaxes(coarse_ref[:, 0], 0, 1))
    rows = [x[r] for r in range(ny)]
    stage[0] = rows[0]
    stage[1] = rows[1]
    stage[3] = rows[ny - 2]
    stage[4] = rows[ny - 1]
    left = jnp.zeros((phases, width), F32)
    right = jnp.zeros((phases, width), F32)
    for r in range(ny):
        turned = rows[r] if r == 0 else pltpu.roll(rows[r], 2 * r, 1)
        left = jnp.where((lane >= 2 * r) & (lane < 2 * r + 2), turned, left)
        low = nz - 2 + 2 * r
        right = jnp.where((lane >= low) & (lane < low + 2), turned, right)
    right = pltpu.roll(right, (2 * ny - (nz - 2)) % width, 1)
    stage[6] = left
    stage[8] = right
    got[SLOTS - 2] = rows[0]
    got[SLOTS - 1] = rows[ny - 1]

    loads[1].wait()
    flat = labels_ref[...].reshape(-1, width).astype(F32).astype(BF16)

    def column(z):
        pick = (lane == z).astype(BF16)
        return lax.dot_general(
            pick, flat, (((1,), (1,)), ((), ())), preferred_element_type=F32
        )

    stage[2, 0:2] = labels_ref[:, 0].astype(F32)
    stage[5, 0:2] = labels_ref[:, 2 * ny - 1].astype(F32)
    stage[7] = column(0)
    stage[9] = column(width - 1)

    pl.semaphore_wait(barrier, len(PARTS))
    copies = []
    for n, ((dy, dz), (s0, s1), (d0, d1)) in enumerate(PARTS):
        copy = pltpu.make_async_remote_copy(
            src_ref=stage.at[s0:s1],
            dst_ref=got.at[d0:d1],
            send_sem=send_sem.at[n],
            recv_sem=recv_sem.at[n],
            device_id=other(dy, dz),
            device_id_type=MESH,
        )
        copy.start()
        copies.append(copy)

    phase_id = lax.broadcasted_iota(jnp.int32, (phases, width), 0)
    rate = jnp.zeros((phases, width), F32)
    loads[2].wait()
    for p in range(phases):
        rate = jnp.where(phase_id == p, STEP * mobility_ref[p], rate)
    rate_ref[...] = rate
    loads[3].wait()
    fine_z = exact_dot(x.reshape(-1, width), main_ref[...]).reshape(ny, phases, width)
    fine_ref[0], fine_ref[2 * ny - 1] = fine_z[0], fine_z[ny - 1]
    for y in range(1, 2 * ny - 1):
        (r0, a), (r1, b) = taps(y)
        fine_ref[y] = a * fine_z[r0] + b * fine_z[r1]
    for n in range(2):
        for y in range(2 * ny):
            label = jnp.broadcast_to(labels_ref[n, y : y + 1], rate.shape)
            pin_ref[n, y] = jnp.where(label == phase_id, rate, 0.0)

    loads[4].wait()
    third = jnp.zeros((phases, width), F32)
    for r in range(ny):
        hit = (lane == (2 * r + 2) % width) | (lane == (2 * r + nz - 3) % width)
        third = jnp.where(hit, pltpu.roll(rows[r], 2 * r, 1) if r else rows[r], third)
    strips_ref[...] = exact_dot(
        jnp.concatenate([left + right, third], axis=1), strip_ref[: 2 * width]
    )
    loads[5].wait()
    edge_lane = jnp.where(phase_id < 4, phase_id, width - 1 - (phase_id - 4))
    edge_labels = lax.dot_general(
        (lane == edge_lane).astype(BF16), flat, (((1,), (1,)), ((), ())), preferred_element_type=F32
    ).astype(BF16)
    from_left = jnp.dot(edge_labels, label_ref[:width], preferred_element_type=F32)
    from_right = jnp.dot(edge_labels, label_ref[width:], preferred_element_type=F32)
    for k in range(4):
        label = from_left[k : k + 1] + from_right[4 + k : 5 + k]
        for n in range(2):
            one = jnp.broadcast_to(label[:, n * width : (n + 1) * width], rate.shape)
            side_pin_ref[k, n] = jnp.where(one == phase_id.astype(F32), rate, 0.0)

    row = lax.broadcasted_iota(jnp.int32, (2 * width, width), 0) % width
    column_id = lax.broadcasted_iota(jnp.int32, (2 * width, width), 1)
    beside = (jnp.abs(row - column_id) == 1).astype(F32).astype(BF16)
    row = lax.broadcasted_iota(jnp.int32, (8 * phases, 16 * phases), 0)
    column_id = lax.broadcasted_iota(jnp.int32, (8 * phases, 16 * phases), 1) % (8 * phases)
    ones = (row // phases == column_id // phases).astype(F32).astype(BF16)
    cur = fine_ref[...]
    near, squares = mixed(cur, beside, ones)
    base = cur + rate * (near + above_below(cur) - cur * (4.0 + squares))
    both = [base + pin_ref[n] for n in range(2)]
    for n in range(2):
        cur = both[n]
        near, squares = mixed(cur, beside, ones)
        near = near + above_below(cur) + 2.0 * both[1 - n]
        inner_ref[n] = cur + rate * (near - cur * (6.0 + squares)) + pin_ref[n]
    for copy in copies:
        copy.wait()


def relax(got, fine, inner, pin, rate_ref, strips_ref, side_pin, main_ref, strip_ref, label_ref, *rest):
    out_hbm, out_ref, out_sem = rest
    fy, phases, width = fine.shape
    ny, nz = fy // 2, width // 2
    shape = (phases, width)
    lane = lax.broadcasted_iota(jnp.int32, shape, 1)
    phase_f = lax.broadcasted_iota(jnp.int32, shape, 0).astype(F32)
    rate = rate_ref[...]
    first, last = lane == 0, lane == width - 1
    ends = first | last

    def turn(v, by):
        return pltpu.roll(v, by % width, 1) if by % width else v

    def total(v):
        return jnp.broadcast_to(jnp.sum(v * v, axis=0, keepdims=True), shape)

    def around(c, side):
        return jnp.where(first, side, turn(c, 1)) + jnp.where(last, side, turn(c, -1))

    halo_right = (lane >= nz) & (lane < nz + 2)
    halo_left = lane >= width - 2

    def edge(row, from_left, from_right, left_by=nz, right_by=nz):
        v = jnp.where(halo_right, turn(from_right, right_by), row)
        return jnp.where(halo_left, turn(from_left, left_by), v)

    below = [edge(got[n], got[12 + n], got[10 + n]) for n in range(2)]
    above = [edge(got[3 + n], got[16 + n], got[14 + n]) for n in range(2)]
    low = 2 * (ny - 1)
    top = edge(got[SLOTS - 2], got[8], got[6], width - 2 - 2 * ny, nz)
    bottom = edge(got[SLOTS - 1], got[8], got[6], width - 2 - 2 * ny - low, nz - low)
    rim_rows = jnp.concatenate([*above, top, bottom, *below], axis=0)
    rim_fine = exact_dot(rim_rows, main_ref[...])
    rim_fine = [rim_fine[n * phases : (n + 1) * phases] for n in range(6)]
    at_rim = dict(zip((-2, -1, 0, ny - 1, ny, ny + 1), rim_fine))

    beside = jnp.where(lane < 2 * ny, got[6], got[8])
    near = (lane < 4) | (lane >= nz - 4) & (lane < nz + 4) | (lane >= width - 4)
    rim = jnp.where(near, above[1], turn(below[0], 8))
    strips = exact_dot(jnp.concatenate([beside, rim], axis=1), strip_ref[2 * width :])
    strips = strips + strips_ref[...]
    blocks = [strips[:, n * width : (n + 1) * width] for n in range(8)]
    corner = blocks.pop(3)
    fine_at = dict(zip(range(-2, 5), blocks))
    near_labels = jnp.concatenate([got[9], got[7]], axis=1).astype(BF16)
    strip_labels = jnp.dot(near_labels, label_ref[...], preferred_element_type=F32)

    def side_pinned(k, n):
        if k >= 0:
            return side_pin[k, n]
        return jnp.where(strip_labels[:, n * width : (n + 1) * width] == phase_f, rate, 0.0)

    step1 = {}
    for k in range(-1, 4):
        c = fine_at[k]
        up, down = turn(c, 2), turn(c, -2)
        if k < 0:
            up = jnp.where(ends, corner, up)
            down = jnp.where((lane == width - 2) | (lane == width - 3), corner, down)
        near = fine_at[k - 1] + fine_at[k + 1] + up + down
        base = c + rate * (near - c * (4.0 + total(c)))
        step1[k] = [base + side_pinned(k, n) for n in range(2)]
    side, side1 = fine_at[-1], step1[-1]
    step2 = {}
    for k in range(3):
        step2[k] = []
        for n in range(2):
            c = step1[k][n]
            near = step1[k - 1][n] + step1[k + 1][n] + turn(c, 2) + turn(c, -2)
            near = near + 2.0 * step1[k][1 - n]
            new = c + rate * (near - c * (6.0 + total(c))) + side_pin[k, n]
            if k:
                new = jnp.where(lane % 2 == k % 2, turn(new, k), turn(new, -k))
            step2[k].append(new)

    def fine_row(y):
        if 0 < y < fy - 1:
            v = fine[y]
        else:
            (r0, a), (r1, b) = taps(y)
            v = a * at_rim[r0] + b * at_rim[r1]
        return jnp.where(ends, turn(fine_at[0], -2 * y), v) if 0 <= y < fy else v

    def pinned(n, y):
        if 0 <= y < fy:
            return pin[n, y]
        row = got[5, n : n + 1] if y < 0 else got[2, n : n + 1]
        return jnp.where(jnp.broadcast_to(row, shape) == phase_f, rate, 0.0)

    def first_row(y):
        prev, cur, nxt = (fine_row(v) for v in (y - 1, y, y + 1))
        if y < 0:
            beside_row = corner
        elif y == fy:
            beside_row = turn(corner, 2)
        else:
            beside_row = turn(side, -2 * y)
        base = cur + rate * (prev + nxt + around(cur, beside_row) - cur * (4.0 + total(cur)))
        return [base + pinned(n, y) for n in range(2)]

    rim1 = {y: first_row(y) for y in (*range(-1, 4), *range(fy - 4, fy + 1))}
    at_column = [(lane == k) | (lane == width - 1 - k) for k in range(3)]

    def second_row(n, y):
        if 3 <= y < fy - 3:
            new = inner[n, y]
            for k in range(3):
                new = jnp.where(at_column[k], turn(step2[k][n], -2 * y), new)
            return new
        c = rim1[y][n]
        near = rim1[y - 1][n] + rim1[y + 1][n] + around(c, turn(side1[n], -2 * y))
        near = near + 2.0 * rim1[y][1 - n]
        return c + rate * (near - c * (6.0 + total(c))) + pinned(n, y)

    chunks, _, _, tall, _ = out_ref.shape
    copies = []
    for chunk in range(chunks):
        for n in range(2):
            for j in range(0, tall, 8):
                rows = jnp.stack([second_row(n, chunk * tall + j + i) for i in range(8)])
                out_ref[chunk, :, n, j : j + 8] = jnp.swapaxes(rows, 0, 1)
        copy = pltpu.make_async_copy(
            out_ref.at[chunk], out_hbm.at[:, :, pl.ds(chunk * tall, tall)], out_sem.at[chunk]
        )
        copy.start()
        copies.append(copy)
    for copy in copies:
        copy.wait()


def shards(gy, gz, coarse, labels, mobility):
    phases, planes, ny, nz = coarse.shape
    assert planes == 1 and labels.shape == (2, 2 * ny, 2 * nz) and ny <= nz // 2 and phases == 8
    width = 2 * nz
    vmem = pl.BlockSpec(memory_space=pltpu.VMEM)
    hbm = pl.BlockSpec(memory_space=pltpu.HBM)
    weights = [
        jnp.asarray(w, BF16)
        for w in (main_operator(nz), strip_operator(ny, nz), label_operator(ny, nz))
    ]
    sources = [pltpu.with_memory_space_constraint(v, pltpu.HBM) for v in (coarse, labels, mobility, *weights)]
    shared = [
        pltpu.VMEM((SLOTS, phases, width), F32),
        pltpu.VMEM((2 * ny, phases, width), F32),
        pltpu.VMEM((2, 2 * ny, phases, width), F32),
        pltpu.VMEM((2, 2 * ny, phases, width), F32),
        pltpu.VMEM((phases, width), F32),
        pltpu.VMEM((phases, 8 * width), F32),
        pltpu.VMEM((4, 2, phases, width), F32),
        *(pltpu.VMEM(v.shape, v.dtype) for v in weights),
    ]
    parts = pl.pallas_call(
        functools.partial(exchange, gy, gz),
        out_shape=shared,
        in_specs=[hbm] * len(sources),
        out_specs=[vmem] * len(shared),
        scratch_shapes=[
            pltpu.SMEM(mobility.shape, F32),
            pltpu.VMEM(labels.shape, jnp.int32),
            pltpu.VMEM(coarse.shape, F32),
            pltpu.VMEM((10, phases, width), F32),
            pltpu.SemaphoreType.DMA((len(PARTS),)),
            pltpu.SemaphoreType.DMA((len(PARTS),)),
            pltpu.SemaphoreType.DMA((len(sources),)),
        ],
        compiler_params=pltpu.CompilerParams(
            collective_id=0, has_side_effects=True, vmem_limit_bytes=12 * 2**20
        ),
        name="exchange",
    )(*sources)
    return pl.pallas_call(
        relax,
        out_shape=jax.ShapeDtypeStruct((phases, 2, 2 * ny, width), F32),
        in_specs=[vmem] * len(shared),
        out_specs=hbm,
        scratch_shapes=[
            pltpu.VMEM((2, phases, 2, ny, width), F32),
            pltpu.SemaphoreType.DMA((2,)),
        ],
        compiler_params=pltpu.CompilerParams(vmem_limit_bytes=12 * 2**20),
        name="relax",
    )(*parts)


def solution(mesh):
    in_specs = (P(None, None, "gy", "gz"), P(None, "gy", "gz"), P())
    out_specs = P(None, None, "gy", "gz")
    fn = functools.partial(shards, mesh.shape["gy"], mesh.shape["gz"])
    return jax.shard_map(fn, mesh=mesh, in_specs=in_specs, out_specs=out_specs, check_vma=False)
```
